512 devices in a mesh: ctx: 32 (over x_lo, z), kv: 8 (over x_hi, y), pb: 2 (over core).
Axes of the slice: x: 4 (x_hi: 2, x_lo: 2; x = x_hi * 2 + x_lo), y: 4, z: 16, core: 2. Of those that a mesh axis runs over, the one named last changes fastest.
Arguments:
- queries: bfloat16 [8, 8, 256, 128], P('kv', None, 'pb'), may hold values from -24 to 24
- cache_keys: bfloat16 [8, 131072, 128], P('kv', 'ctx'), may hold values from -6 to 6
- cache_values: bfloat16 [8, 131072, 128], P('kv', 'ctx'), may hold values from -6 to 6
- sel_index: int32 [8, 2048], P('kv', 'ctx'), may hold values from 0 to 131071, as said below
Outputs:
- gram: float32 [8, 2048, 2048], P('kv', ('ctx', 'pb'))
- value_rhs: float32 [8, 2048, 128], P('kv', ('ctx', 'pb'))
- mass_gap: float32 [8, 8, 256], P('kv', None, 'pb')
The draws below stay inside these ranges and needn't reach their ends.
Inputs may be any that keep to these rules, and one draw needn't show every extreme that they name: `sel_index`: for every KV head, entries k * 64 to (k + 1) * 64 - 1 are distinct positions of context block k (from k * 4096 to (k + 1) * 4096 - 1), in increasing order.
All inputs are finite; a program needn't handle non-finite values.
Results may differ from the reference program's by a relative error of at most 0.0016.
Values may be sent and summed in bfloat16 or wider, within the bound.
No kernel may reach another device: no remote copies, remote signals or barrier semaphores. Data moves between devices by JAX's collectives and lax.ppermute only.
A program may use at most 64 MiB of HBM per device.

```python
import jax
import jax.numpy as jnp
from jax import lax

HD = 128
G = 8
CTX_DEV = 4096
SEL_DEV = 64
KVH = 8
CTX = 131072
SEL = 2048
R = 256


def selection(key):
    base = jax.random.fold_in(key, 4099)
    blocks = CTX // CTX_DEV
    subkeys = jax.random.split(base, KVH * blocks)
    picks = jax.vmap(lambda sub: jnp.sort(jax.random.permutation(sub, CTX_DEV)[:SEL_DEV]))(subkeys)
    offsets = jnp.arange(KVH * blocks, dtype=jnp.int32) % blocks * CTX_DEV
    return (picks.astype(jnp.int32) + offsets[:, None]).reshape(KVH, SEL_DEV * blocks).astype(jnp.int32)


def draw_sel_index(key, part):
    return selection(key)


def draw_cache_keys(key, part):
    inner = jax.random.fold_in(key, 17)
    base = jnp.clip(jax.random.normal(inner, (KVH, CTX, HD), jnp.float32), -6.0, 6.0)
    return base.astype(jnp.bfloat16)


def draw_queries(key, part):
    inner = jax.random.fold_in(key, 29)
    base = jnp.clip(jax.random.normal(inner, (KVH, G, R, HD), jnp.float32), -6.0, 6.0)
    return base.astype(jnp.bfloat16)


def steps_of(key, extent, pieces, low, high):
    level, own = 1.0, jax.random.fold_in(key, 6)
    for axis_at, blocks in pieces:
        heights = jnp.exp(jax.random.uniform(jax.random.fold_in(own, axis_at), (blocks,), jnp.float32, low / len(pieces), high / len(pieces)))
        level = level * jnp.repeat(heights, extent[axis_at] // blocks).reshape([-1 if axis == axis_at else 1 for axis in range(len(extent))])
    return level


def gaussian(key, extent, scale, bound, pieces=(), held_as=jnp.bfloat16):
    loudness = steps_of(key, extent, pieces, -0.22, 0.18) if pieces else 1.0
    values = jax.random.normal(key, extent, jnp.float32) * scale * loudness
    return jnp.minimum(jnp.maximum(values, -bound), bound).astype(held_as)


def setup_inputs(seed: int = 0) -> dict:
    seeds = jax.random.split(jax.random.key(seed), 5)
    queries = draw_queries(jax.random.fold_in(seeds[4], 71), 0)
    cache_keys = draw_cache_keys(jax.random.fold_in(seeds[4], 71), 0)
    cache_values = gaussian(seeds[2], (KVH, CTX, HD), 1.0, 6.0, ((0, 8), (1, 32)))
    sel_index = draw_sel_index(jax.random.fold_in(seeds[4], 71), 0)
    return dict(queries=queries, cache_keys=cache_keys, cache_values=cache_values, sel_index=sel_index)


eps = 1e-06

def head_terms(inputs):
    query, keys, values, index = inputs
    width = query.shape[-1]
    scale = width ** (-0.5)
    rows = query.reshape(-1, width)
    blocks = CTX // CTX_DEV
    key_blocks = keys.reshape(blocks, CTX_DEV, width)
    value_blocks = values.reshape(blocks, CTX_DEV, width)

    def one_block(carry, pair):
        key_block, value_block = pair
        scores = jnp.dot(rows, key_block.T, preferred_element_type=jnp.float32) * scale
        block_max = lax.optimization_barrier(jnp.max(scores, axis=1))
        expo = jnp.exp(scores - block_max[:, None])
        block_total = lax.optimization_barrier(jnp.sum(expo, axis=1))
        block_out = jnp.dot(expo.astype(jnp.bfloat16), value_block, preferred_element_type=jnp.float32)
        return (carry, (block_max, block_total, block_out))
    _, (maxima, totals, outs) = lax.scan(one_block, jnp.float32(0.0), (key_blocks, value_blocks))
    top = lax.optimization_barrier(jnp.max(maxima, axis=0))
    weight = jnp.exp(maxima - top[None, :])
    total = lax.optimization_barrier(jnp.sum(weight * totals, axis=0))
    summed = lax.optimization_barrier(jnp.sum(weight[:, :, None] * outs, axis=0))
    target = summed / total[:, None]
    target_y = (target * lax.rsqrt(lax.optimization_barrier(jnp.mean(target * target, axis=1, keepdims=True)) + eps)).astype(jnp.bfloat16)
    compact = jnp.take(keys, index.astype(jnp.int32), axis=0)
    cscores = jnp.dot(rows, compact.T, preferred_element_type=jnp.float32) * scale
    cmax = lax.optimization_barrier(jnp.max(cscores, axis=1))
    cexp = jnp.exp(cscores - cmax[:, None])
    ctotal = lax.optimization_barrier(jnp.sum(cexp, axis=1))
    feat = (SEL * cexp / ctotal[:, None]).astype(jnp.bfloat16)
    inverse = 1.0 / (G * R)
    gram = jnp.dot(feat.T, feat, preferred_element_type=jnp.float32) * inverse
    value_rhs = jnp.dot(feat.T, target_y, preferred_element_type=jnp.float32) * inverse
    mass_gap = (top + jnp.log(total) - (cmax + jnp.log(ctotal))).reshape(G, R)
    return (gram, value_rhs, mass_gap)

def reference(queries, cache_keys, cache_values, sel_index):
    gram, value_rhs, mass_gap = lax.map(head_terms, (queries, cache_keys, cache_values, sel_index))
    return (gram, value_rhs, mass_gap)
```

```python
import functools
import math

import jax
import jax.numpy as jnp
from jax import lax
from jax.experimental import pallas as pl
from jax.experimental.pallas import tpu as pltpu
from jax.sharding import PartitionSpec as P

eps = 1e-06
LOG2E = math.log2(math.e)
F32, BF16 = jnp.float32, jnp.bfloat16
VMEM = pl.BlockSpec(memory_space=pltpu.VMEM)
NT = (((1,), (1,)), ((), ()))


def call(name, body, outs, ins, scratch=(), after=(), flops=0, exps=0, moved=0, limit=48):
    count, skip = len(ins), len(after)

    def ordered(*refs):
        body(*refs[:count], *refs[count + skip :])

    return pl.pallas_call(
        ordered,
        name=name,
        out_shape=[jax.ShapeDtypeStruct(s, d) for s, d in outs],
        in_specs=[VMEM] * count + [pl.BlockSpec(memory_space=pl.ANY)] * skip,
        out_specs=[VMEM] * len(outs),
        scratch_shapes=list(scratch),
        compiler_params=pltpu.CompilerParams(vmem_limit_bytes=limit << 20),
        cost_estimate=pl.CostEstimate(flops=flops, transcendentals=exps, bytes_accessed=moved),
    )(*ins, *after)


def split3(x):
    hi = x.astype(BF16)
    rest = x - hi.astype(F32)
    mid = rest.astype(BF16)
    low = (rest - mid.astype(F32)).astype(BF16)
    return hi, mid, low


def joined3(a, b, c):
    return (a.astype(F32) + b.astype(F32)) + c.astype(F32)


def pick_body(sel_ref, keys_ref, out_ref):
    peers, half, _ = out_ref.shape
    count = sel_ref.shape[1]
    tokens = keys_ref.shape[0]
    base = lax.axis_index("ctx") * tokens
    first = lax.axis_index("pb") * half
    row = lax.broadcasted_iota(jnp.int32, (half, count), 0) + first
    lane = lax.broadcasted_iota(jnp.int32, (half, count), 1)
    sel = jnp.broadcast_to((sel_ref[...] - base).astype(F32), (half, count))
    col = jnp.sum(jnp.where(row == lane, sel, 0.0), axis=1, keepdims=True).astype(jnp.int32)
    step = 512
    acc = jnp.zeros((half, keys_ref.shape[1]), F32)
    for k in range(0, tokens, step):
        at = lax.broadcasted_iota(jnp.int32, (half, step), 1) + k
        hot = (at == col).astype(F32).astype(BF16)
        acc += jnp.dot(hot, keys_ref[k : k + step, :], preferred_element_type=F32)
    mine = acc.astype(BF16)
    for p in range(peers):
        out_ref[p] = mine


def attend_body(rt, q_ref, k_ref, v_ref, out_ref, s_ref, m_ref):
    rows, width = q_ref.shape
    tokens = k_ref.shape[0]
    tiles = rows // rt
    step = 512
    c = LOG2E * width**-0.5
    share = rows // out_ref.shape[0]

    def scores(t, slot, k):
        q = q_ref[pl.ds(pl.multiple_of(t * rt, rt), rt), :]
        s = lax.dot_general(q, k_ref[k : k + step, :], NT, preferred_element_type=F32)
        s_ref[slot, :, k : k + step] = s
        mx = s[:, :128]
        for j in range(128, step, 128):
            mx = jnp.maximum(mx, s[:, j : j + 128])
        return mx

    def weighed(slot, k, mc, acc):
        l, o = acc
        p = jnp.exp2(s_ref[slot, :, k : k + step] * c - mc)
        for j in range(0, step, 128):
            l = l + p[:, j : j + 128]
        o = o + jnp.dot(p.astype(BF16), v_ref[k : k + step, :], preferred_element_type=F32)
        return l, o

    def close(t, mc, acc):
        l, o = acc
        total = jnp.sum(l, axis=1, keepdims=True)
        o = (o / total).astype(BF16)
        lse = (mc + jnp.log2(total)) * (1.0 / LOG2E)
        lanes = jnp.broadcast_to(lse, (rt, 128))
        for g in range(rt // 128):
            line = lanes[g * 128 : (g + 1) * 128, :].T[:16, :]
            hi, mid, low = split3(line)
            r = lax.broadcasted_iota(jnp.int32, (16, 128), 0)
            three = jnp.where(r == 0, hi.astype(F32), jnp.where(r == 1, mid.astype(F32), low.astype(F32)))
            three = three.astype(BF16)
            for j in range(128 // share):
                p = t * (rt // share) + g * (128 // share) + j
                out_ref[p, 0:share, :] = o[g * 128 + j * share : g * 128 + (j + 1) * share, :]
                out_ref[p, share : share + 16, :] = three

    def maxed(mx):
        return jnp.max(mx, axis=1, keepdims=True) * c

    def zero():
        return jnp.zeros((rt, 128), F32), jnp.zeros((rt, width), F32)

    mx = scores(0, 0, 0)
    for k in range(step, tokens, step):
        mx = jnp.maximum(mx, scores(0, 0, k))
    m_ref[...] = jnp.broadcast_to(maxed(mx), (rt, 128))

    def loop(t, carry):
        slot = t % 2
        mc = m_ref[:, :1]
        acc, mx = zero(), None
        for k in range(0, tokens, step):
            new = scores(t + 1, 1 - slot, k)
            mx = new if mx is None else jnp.maximum(mx, new)
            acc = weighed(slot, k, mc, acc)
        close(t, mc, acc)
        m_ref[...] = jnp.broadcast_to(maxed(mx), (rt, 128))
        return carry

    lax.fori_loop(0, tiles - 1, loop, 0)
    last = tiles - 1
    mc = m_ref[:, :1]
    acc = zero()
    for k in range(0, tokens, step):
        acc = weighed(last % 2, k, mc, acc)
    close(last, mc, acc)


def features_body(rt, q_ref, mine_ref, other_ref, keep_ref, send_ref, own_ref, stat_ref, c_ref, f_ref):
    rows, width = q_ref.shape
    peers, half, _ = mine_ref.shape
    count = 2 * half
    sel = peers * count
    c = LOG2E * width**-0.5
    pb = lax.axis_index("pb")
    at = lax.axis_index("ctx")
    for j in range(peers):
        c_ref[pl.ds(pl.multiple_of(j * count + pb * half, half), half), :] = mine_ref[j]
        c_ref[pl.ds(pl.multiple_of(j * count + (1 - pb) * half, half), half), :] = other_ref[j]
    for t in range(rows // rt):
        s = lax.dot_general(c_ref[...], q_ref[t * rt : (t + 1) * rt, :], NT, preferred_element_type=F32)
        mx = jnp.max(s, axis=0, keepdims=True) * c
        e = jnp.exp2(s * c - mx)
        total = jnp.sum(e, axis=0, keepdims=True)
        f_ref[:, t * rt : (t + 1) * rt] = (e * (sel / total)).astype(BF16)
        stat = (mx + jnp.log2(total)) * (1.0 / LOG2E)
        for g in range(rt // 128):
            r = t * (rt // 128) + g
            stat_ref[r : r + 1, :] = stat[:, g * 128 : (g + 1) * 128]
    own_ref[:half, :] = f_ref[pl.ds(pl.multiple_of(at * count + pb * half, half), half), :]
    own_ref[half:, :] = f_ref[pl.ds(pl.multiple_of(at * count + (1 - pb) * half, half), half), :]
    step = 512
    for k in range(0, sel, step):
        g = lax.dot_general(own_ref[...], f_ref[k : k + step, :], NT, preferred_element_type=F32)
        g = g * (1.0 / (2 * rows))
        keep_ref[:, k : k + step] = g[:half]
        send_ref[:, k : k + step] = g[half:]


def settle_body(in_ref, out_ref, w_ref):
    peers = in_ref.shape[0]
    share = in_ref.shape[1] - 16
    at = lax.axis_index("ctx")
    first = (at % (128 // share)) * share
    lines = in_ref[:, share : share + 16, :].astype(F32)
    lse = (lines[:, 0, :] + lines[:, 1, :]) + lines[:, 2, :]
    top = jnp.max(lse, axis=0, keepdims=True)
    w = jnp.exp(lse - top)
    total = jnp.sum(w, axis=0, keepdims=True)
    w = w / total
    pad = jnp.concatenate([w, jnp.zeros((128 - peers, 128), F32)], axis=0) if peers < 128 else w
    w_ref[...] = pad.T
    mine = w_ref[pl.ds(pl.multiple_of(first, share), share), :]
    acc = jnp.zeros((share, 128), F32)
    for b in range(peers):
        acc = acc + mine[:, b : b + 1] * in_ref[b, :share, :].astype(F32)
    y = (acc * lax.rsqrt(jnp.mean(acc * acc, axis=1, keepdims=True) + eps)).astype(BF16)
    full = jnp.broadcast_to(top + jnp.log(total), (16, 128))
    hi, mid, low = split3(full)
    r = lax.broadcasted_iota(jnp.int32, (16, 128), 0)
    three = jnp.where(r == 0, hi.astype(F32), jnp.where(r == 1, mid.astype(F32), low.astype(F32))).astype(BF16)
    for p in range(peers):
        out_ref[p, :share, :] = y
        out_ref[p, share : share + 16, :] = three


def rhs_body(in_ref, own_ref, stat_ref, keep_ref, send_ref, gap_ref, y_ref):
    peers = in_ref.shape[0]
    share = in_ref.shape[1] - 16
    half = keep_ref.shape[0]
    rows = peers * share
    for p in range(peers):
        y_ref[p * share : (p + 1) * share, :] = in_ref[p, :share, :]
    g = jnp.dot(own_ref[...], y_ref[...], preferred_element_type=F32) * (1.0 / (2 * rows))
    keep_ref[...] = g[:half]
    send_ref[...] = g[half:]
    per = 128 // share
    lane = lax.broadcasted_iota(jnp.int32, (1, 128), 1)
    for h in range(rows // 128):
        line = jnp.zeros((1, 128), F32)
        for j in range(per):
            x = in_ref[h * per + j, share : share + 16, :].astype(F32)
            v = (x[0:1] + x[1:2]) + x[2:3]
            line = jnp.where((lane >= j * share) & (lane < (j + 1) * share), v, line)
        gap_ref[h : h + 1, :] = line - stat_ref[h : h + 1, :]


def shards(queries, cache_keys, cache_values, sel_index):
    heads, rows_dev, width = queries.shape[1:]
    q = queries[0].reshape(-1, width)
    keys, values = cache_keys[0], cache_values[0]
    rows, tokens = q.shape[0], keys.shape[0]
    peers = lax.axis_size("ctx")
    share = rows // peers
    count = sel_index.shape[1]
    half = count // 2
    sel = count * peers
    swap = [(0, 1), (1, 0)]

    def exchange(x):
        return lax.all_to_all(x, "ctx", 0, 0, tiled=True)

    (picked,) = call(
        "pick", pick_body, [((peers, half, width), BF16)], (sel_index, keys), flops=2 * half * tokens * width, moved=tokens * width * 2
    )
    mine = exchange(picked)
    rt = 256
    (parts,) = call(
        "attend",
        functools.partial(attend_body, rt),
        [((peers, share + 16, width), BF16)],
        (q, keys, values),
        after=(picked,),
        scratch=[pltpu.VMEM((2, rt, tokens), F32), pltpu.VMEM((rt, 128), F32)],
        flops=4 * rows * tokens * width,
        exps=rows * tokens,
        moved=tokens * width * 4,
    )
    arrived = exchange(parts)
    other = lax.ppermute(mine, "pb", swap)
    keep, send, own, stat = call(
        "features",
        functools.partial(features_body, rt),
        [((half, sel), F32), ((half, sel), F32), ((count, rows), BF16), ((rows // 128, 128), F32)],
        (q, mine, other),
        after=(parts,),
        scratch=[pltpu.VMEM((sel, width), BF16), pltpu.VMEM((sel, rows), BF16)],
        flops=2 * rows * sel * width + 2 * count * rows * sel,
        exps=rows * sel,
        moved=sel * width * 4,
    )
    (told,) = call(
        "settle",
        settle_body,
        [((peers, share + 16, width), BF16)],
        (arrived,),
        after=(stat,),
        scratch=[pltpu.VMEM((128, 128), F32)],
        flops=4 * rows * width,
        moved=2 * rows * width * 2,
    )
    heard = exchange(told)
    gram = keep + lax.ppermute(send, "pb", swap)
    rkeep, rsend, gap = call(
        "rhs",
        rhs_body,
        [((half, width), F32), ((half, width), F32), ((rows // 128, 128), F32)],
        (heard, own, stat),
        scratch=[pltpu.VMEM((rows, width), BF16)],
        flops=2 * count * rows * width,
        moved=rows * width * 2,
    )
    rhs = rkeep + lax.ppermute(rsend, "pb", swap)
    return (gram[None], rhs[None], gap.reshape(1, heads, rows_dev))


def solution(mesh):
    in_specs = (
        P("kv", None, "pb", None),
        P("kv", "ctx", None),
        P("kv", "ctx", None),
        P("kv", "ctx"),
    )
    out_specs = (P("kv", ("ctx", "pb"), None), P("kv", ("ctx", "pb"), None), P("kv", None, "pb"))
    return jax.shard_map(shards, mesh=mesh, in_specs=in_specs, out_specs=out_specs, check_vma=False)
```

```python
import functools
import math

import jax
import jax.numpy as jnp
from jax import lax
from jax.experimental import pallas as pl
from jax.experimental.pallas import tpu as pltpu
from jax.sharding import PartitionSpec as P

eps = 1e-06
LOG2E = math.log2(math.e)
F32, BF16 = jnp.float32, jnp.bfloat16
VMEM = pl.BlockSpec(memory_space=pltpu.VMEM)
ANY = pl.BlockSpec(memory_space=pl.ANY)
NT = (((1,), (1,)), ((), ()))
TT = (((0,), (0,)), ((), ()))
STAT = 16


def call(name, body, outs, ins, scratch=(), after=(), held=None, specs=(), flops=0, exps=0, moved=0, limit=20):
    count, skip, here = len(ins), len(after) + (held is not None), len(outs)
    more = [held] if held is not None else []

    def ordered(*refs):
        body(*refs[:count], *refs[count + skip : count + skip + here], *refs[count + skip + here + len(more) :])

    return pl.pallas_call(
        ordered,
        name=name,
        out_shape=[jax.ShapeDtypeStruct(s, d) for s, d in outs] + [jax.ShapeDtypeStruct(m.shape, m.dtype) for m in more],
        in_specs=(list(specs) or [VMEM] * count) + [ANY] * skip,
        out_specs=[VMEM] * here + [ANY] * len(more),
        input_output_aliases={count + skip - 1: here} if more else {},
        scratch_shapes=list(scratch),
        compiler_params=pltpu.CompilerParams(vmem_limit_bytes=limit << 20),
        cost_estimate=pl.CostEstimate(flops=flops, transcendentals=exps, bytes_accessed=moved),
    )(*ins, *after, *more)


def split3(x):
    hi = x.astype(BF16)
    rest = x - hi.astype(F32)
    mid = rest.astype(BF16)
    low = (rest - mid.astype(F32)).astype(BF16)
    return hi, mid, low


def joined3(a, b, c):
    return (a.astype(F32) + b.astype(F32)) + c.astype(F32)


def packed3(line):
    hi, mid, low = split3(jnp.broadcast_to(line, (STAT, 128)))
    r = lax.broadcasted_iota(jnp.int32, (STAT, 128), 0)
    return jnp.where(r == 0, hi.astype(F32), jnp.where(r == 1, mid.astype(F32), low.astype(F32))).astype(BF16)


def column(line):
    return jnp.broadcast_to(line, (128, 128)).T


def place(ring):
    at = lax.axis_index("ctx")
    return at // ring, at % ring


def attend(ring, away, q_hbm, k_hbm, v_hbm, q_ref, k_ref, v_ref, s_ref, sem):
    rows, width = q_ref.shape
    tokens = k_ref.shape[0]
    step = 512
    c = LOG2E * width**-0.5
    x, _ = place(ring)
    part = 1 - x if away else x
    copies = [pltpu.make_async_copy(q_hbm.at[pl.ds(pl.multiple_of(part * rows, rows), rows)], q_ref, sem.at[0])]
    for ref, hbm in ((k_ref, k_hbm), (v_ref, v_hbm)):
        for a in range(0, tokens, step):
            cut = pl.ds(a, step)
            copies.append(pltpu.make_async_copy(hbm.at[cut], ref.at[cut], sem.at[len(copies)]))
    for copy in copies:
        copy.start()
    copies[0].wait()
    q = q_ref[...]
    chunks = tokens // step
    mx = None
    for n in range(chunks):
        copies[1 + n].wait()
        a = n * step
        s = lax.dot_general(k_ref[a : a + step, :], q, NT, preferred_element_type=F32)
        s_ref[a : a + step, :] = s
        top = jnp.max(s.reshape(step // 8, 8, rows), axis=0)
        mx = top if mx is None else jnp.maximum(mx, top)
    mc = jnp.max(mx, axis=0, keepdims=True) * c
    total, out = jnp.zeros((8, rows), F32), jnp.zeros((width, rows), F32)
    for n in range(chunks):
        copies[1 + chunks + n].wait()
        a = n * step
        p = jnp.exp2(s_ref[a : a + step, :] * c - mc)
        total = total + jnp.sum(p.reshape(step // 8, 8, rows), axis=0)
        out = out + lax.dot_general(v_ref[a : a + step, :], p.astype(BF16), TT, preferred_element_type=F32)
    total = jnp.sum(total, axis=0, keepdims=True)
    return (out * (1.0 / total)).T, (mc + jnp.log2(total)) * (1.0 / LOG2E)


def away_body(ring, sel_hbm, q_hbm, k_hbm, v_hbm, out_ref, pick_ref, sel_ref, q_ref, k_ref, v_ref, s_ref, sem, sel_sem):
    fetch = pltpu.make_async_copy(sel_hbm, sel_ref, sel_sem)
    fetch.start()
    o, lse = attend(ring, True, q_hbm, k_hbm, v_hbm, q_ref, k_ref, v_ref, s_ref, sem)
    rows, width = q_ref.shape
    tokens = k_ref.shape[0]
    share = rows // ring
    per = 128 // share
    o = o.astype(BF16)
    block = share + STAT
    for g in range(rows // 128):
        three = packed3(lse[:, g * 128 : (g + 1) * 128])
        for j in range(g * per, (g + 1) * per):
            out_ref[j * block : j * block + share, :] = o[j * share : (j + 1) * share, :]
            out_ref[j * block + share : (j + 1) * block, :] = three
    fetch.wait()
    half = pick_ref.shape[0]
    count = sel_ref.shape[1]
    base = lax.axis_index("ctx") * tokens
    first = lax.axis_index("pb") * half
    row = lax.broadcasted_iota(jnp.int32, (half, count), 0) + first
    lane = lax.broadcasted_iota(jnp.int32, (half, count), 1)
    sel = jnp.broadcast_to((sel_ref[...] - base).astype(F32), (half, count))
    col = jnp.sum(jnp.where(row == lane, sel, 0.0), axis=1, keepdims=True).astype(jnp.int32)
    step = 512
    acc = jnp.zeros((half, width), F32)
    for k in range(0, tokens, step):
        at = lax.broadcasted_iota(jnp.int32, (half, step), 1) + k
        hot = (at == col).astype(F32).astype(BF16)
        acc += jnp.dot(hot, k_ref[k : k + step, :], preferred_element_type=F32)
    mine = acc.astype(BF16)
    pick_ref[...] = mine
    out_ref[ring * block : ring * block + half, :] = mine


def home_body(ring, q_hbm, k_hbm, v_hbm, out_ref, lse_ref, q_ref, k_ref, v_ref, s_ref, sem):
    o, lse = attend(ring, False, q_hbm, k_hbm, v_hbm, q_ref, k_ref, v_ref, s_ref, sem)
    out_ref[...] = o
    lse_ref[...] = jnp.zeros_like(lse_ref)
    for g in range(o.shape[0] // 128):
        lse_ref[g : g + 1, :] = lse[:, g * 128 : (g + 1) * 128]


def pair_body(o_ref, lse_ref, in_ref, pick_ref, out_ref):
    ring = out_ref.shape[0]
    rows = o_ref.shape[0]
    half = pick_ref.shape[0]
    share = rows // ring
    per = 128 // share
    block = share + STAT
    mine, theirs = pick_ref[...], in_ref[ring * block : ring * block + half, :]
    for g in range(rows // 128):
        at = g * per * block
        three = in_ref[at + share : at + block, :].astype(F32)
        other = (three[0:1] + three[1:2]) + three[2:3]
        here = lse_ref[g : g + 1, :]
        top = jnp.maximum(other, here)
        wo, wh = jnp.exp(other - top), jnp.exp(here - top)
        total = wo + wh
        lines = packed3(top + jnp.log(total))
        share_of = column(wh / total)
        for j in range(g * per, (g + 1) * per):
            w = share_of[(j % per) * share : (j % per + 1) * share, :]
            a = in_ref[j * block : j * block + share, :].astype(F32)
            h = o_ref[j * share : (j + 1) * share, :]
            out_ref[j, :share, :] = (a + w * (h - a)).astype(BF16)
            out_ref[j, share:block, :] = lines
            out_ref[j, block : block + half, :] = mine
            out_ref[j, block + half :, :] = theirs


def settle_body(share, in_ref, out_ref, keys_ref, w_ref):
    ring = in_ref.shape[0]
    block = share + STAT
    _, z = place(ring)
    lines = in_ref[:, share:block, :].astype(F32)
    lse = (lines[:, 0, :] + lines[:, 1, :]) + lines[:, 2, :]
    top = jnp.max(lse, axis=0, keepdims=True)
    w = jnp.exp(lse - top)
    total = jnp.sum(w, axis=0, keepdims=True)
    w = w / total
    w_ref[...] = jnp.concatenate([w, jnp.zeros((128 - ring, 128), F32)], axis=0).T
    mine = w_ref[pl.ds(pl.multiple_of((z % (128 // share)) * share, share), share), :]
    acc = jnp.zeros((share, 128), F32)
    for b in range(ring):
        acc = acc + mine[:, b : b + 1] * in_ref[b, :share, :].astype(F32)
    y = (acc * lax.rsqrt(jnp.mean(acc * acc, axis=1, keepdims=True) + eps)).astype(BF16)
    three = packed3(top + jnp.log(total))
    for p in range(ring):
        out_ref[p, :share, :] = y
        out_ref[p, share:, :] = three
        keys_ref[p] = in_ref[p, block:, :]


def features_body(rt, q_ref, mine_ref, other_ref, own_ref, stat_ref, keep_ref, send_ref, c_ref, f_ref, g_ref):
    rows, width = q_ref.shape
    ring, count, _ = mine_ref.shape
    half = count // 2
    sel = 2 * ring * count
    c = LOG2E * width**-0.5
    pb = lax.axis_index("pb")
    x, z = place(ring)
    for j in range(ring):
        for ref, core in ((mine_ref, pb), (other_ref, 1 - pb)):
            for k, side in ((0, x), (1, 1 - x)):
                at = pl.multiple_of((side * ring + j) * count + core * half, half)
                c_ref[pl.ds(at, half), :] = ref[j, k * half : (k + 1) * half, :]
    for t in range(rows // rt):
        s = lax.dot_general(c_ref[...], q_ref[t * rt : (t + 1) * rt, :], NT, preferred_element_type=F32)
        mx = jnp.max(s, axis=0, keepdims=True) * c
        e = jnp.exp2(s * c - mx)
        total = jnp.sum(e, axis=0, keepdims=True)
        f_ref[:, t * rt : (t + 1) * rt] = (e * (sel / total)).astype(BF16)
        stat = (mx + jnp.log2(total)) * (1.0 / LOG2E)
        for g in range(rt // 128):
            r = t * (rt // 128) + g
            stat_ref[r : r + 1, :] = stat[:, g * 128 : (g + 1) * 128]
    there = rows // 2
    lanes = pl.ds(pl.multiple_of(x * there, there), there)
    for k, side in ((0, x), (1, 1 - x)):
        at = pl.multiple_of((side * ring + z) * count, count)
        own_ref[k * count : (k + 1) * count, :] = f_ref[pl.ds(at, count), lanes]
    at = lax.axis_index("ctx") * count
    g_ref[:half, :] = f_ref[pl.ds(pl.multiple_of(at + pb * half, half), half), :]
    g_ref[half:, :] = f_ref[pl.ds(pl.multiple_of(at + (1 - pb) * half, half), half), :]
    step = 512
    for k in range(0, sel, step):
        g = lax.dot_general(g_ref[...], f_ref[k : k + step, :], NT, preferred_element_type=F32)
        g = g * (1.0 / (2 * rows))
        keep_ref[:, k : k + step] = g[:half]
        send_ref[:, k : k + step] = g[half:]


def rhs_body(total_rows, in_ref, own_ref, keep_ref, send_ref, y_ref):
    ring, block, _ = in_ref.shape
    share = block - STAT
    count = keep_ref.shape[0]
    rows = ring * share
    for p in range(ring):
        y_ref[p * share : (p + 1) * share, :] = in_ref[p, :share, :]
    g = jnp.dot(own_ref[...], y_ref[...], preferred_element_type=F32) * (1.0 / total_rows)
    keep_ref[...] = g[:count]
    send_ref[:count, :] = g[count:]
    send_ref[count:, :] = jnp.zeros((8, 128), F32)
    per = 128 // share
    lane = lax.broadcasted_iota(jnp.int32, (1, 128), 1)
    for h in range(rows // 128):
        line = jnp.zeros((1, 128), F32)
        for j in range(per):
            v = in_ref[h * per + j, share:block, :].astype(F32)
            v = (v[0:1] + v[1:2]) + v[2:3]
            line = jnp.where((lane >= j * share) & (lane < (j + 1) * share), v, line)
        send_ref[count + h : count + h + 1, :] = line


def sides_body(ring, keep_ref, sent_ref, got_ref, stat_ref, mine_ref, other_ref, gap_ref, sum_ref):
    count = keep_ref.shape[0]
    half = count // 2
    pb = lax.axis_index("pb")
    x, _ = place(ring)
    sum_ref[...] = keep_ref[...] + got_ref[:count, :]
    mine_ref[...] = sum_ref[pl.ds(pl.multiple_of(pb * half, half), half), :]
    other_ref[...] = sum_ref[pl.ds(pl.multiple_of((1 - pb) * half, half), half), :]
    lines = gap_ref.shape[0] // 2
    here, there = sent_ref[count : count + lines, :], got_ref[count : count + lines, :]
    low = jnp.where(x == 0, here, there)
    high = jnp.where(x == 0, there, here)
    gap_ref[:lines, :] = low - stat_ref[:lines, :]
    gap_ref[lines:, :] = high - stat_ref[lines:, :]


def last_body(a_ref, b_ref, out_ref):
    out_ref[...] = a_ref[...] + b_ref[...]


def shards(queries, cache_keys, cache_values, sel_index):
    heads, rows_dev, width = queries.shape[1:]
    q = queries[0].reshape(-1, width)
    keys, values = cache_keys[0], cache_values[0]
    rows, tokens = q.shape[0], keys.shape[0]
    blocks = lax.axis_size("ctx")
    ring = blocks // 2
    part = rows // 2
    share = part // ring
    block = share + STAT
    count = sel_index.shape[1]
    half = count // 2
    sel = count * blocks
    total_rows = 2 * rows
    swap = [(0, 1), (1, 0)]
    across = [(i, (i + ring) % blocks) for i in range(blocks)]
    rings = [list(range(ring)), list(range(ring, blocks))]

    def exchange(x):
        return lax.all_to_all(x, "ctx", 0, 0, axis_index_groups=rings, tiled=True)

    held = [
        pltpu.VMEM((part, width), BF16),
        pltpu.VMEM((tokens, width), BF16),
        pltpu.VMEM((tokens, width), BF16),
        pltpu.VMEM((tokens, part), F32),
        pltpu.SemaphoreType.DMA((1 + 2 * (tokens // 512),)),
    ]
    work = dict(flops=4 * part * tokens * width, exps=part * tokens, moved=tokens * width * 4, limit=60)
    away, picked = call(
        "away",
        functools.partial(away_body, ring),
        [((ring * block + half, width), BF16), ((half, width), BF16)],
        (sel_index, q, keys, values),
        specs=[ANY] * 4,
        scratch=[pltpu.VMEM((1, count), jnp.int32), *held, pltpu.SemaphoreType.DMA],
        **work,
    )
    came = lax.ppermute(away, "ctx", across)
    home, lse = call(
        "home",
        functools.partial(home_body, ring),
        [((part, width), F32), ((8, 128), F32)],
        (q, keys, values),
        specs=[ANY] * 3,
        after=(picked,),
        scratch=held,
        **work,
    )
    (parts,) = call("pair", pair_body, [((ring, block + count, width), BF16)], (home, lse, came, picked), moved=part * width * 12)
    told, mine = call(
        "settle",
        functools.partial(settle_body, share),
        [((ring, block, width), BF16), ((ring, count, width), BF16)],
        (exchange(parts),),
        scratch=[pltpu.VMEM((128, 128), F32)],
        moved=part * width * 8,
    )
    heard = exchange(told)
    other = lax.ppermute(mine, "pb", swap)
    own, stat, gkeep, gsend = call(
        "features",
        functools.partial(features_body, 256),
        [((2 * count, part), BF16), ((rows // 128, 128), F32), ((half, sel), F32), ((half, sel), F32)],
        (q, mine, other),
        after=(told,),
        scratch=[pltpu.VMEM((sel, width), BF16), pltpu.VMEM((sel, rows), BF16), pltpu.VMEM((count, rows), BF16)],
        flops=2 * rows * sel * (width + count),
        exps=rows * sel,
        moved=sel * width * 4,
    )
    rkeep, rsend, gsend = call(
        "rhs",
        functools.partial(rhs_body, total_rows),
        [((count, width), F32), ((count + 8, width), F32)],
        (heard, own),
        held=gsend,
        scratch=[pltpu.VMEM((part, width), BF16)],
        flops=4 * count * part * width,
        moved=part * width * 2,
    )
    rmine, rother, gap = call(
        "sides",
        functools.partial(sides_body, ring),
        [((half, width), F32), ((half, width), F32), ((rows // 128, 128), F32)],
        (rkeep, rsend, lax.ppermute(rsend, "ctx", across), stat),
        scratch=[pltpu.VMEM((count, width), F32)],
        moved=count * width * 16,
    )
    gram = gkeep + lax.ppermute(gsend, "pb", swap)
    rgot = lax.ppermute(rother, "pb", swap)
    (rhs,) = call("last", last_body, [((half, width), F32)], (rmine, rgot), after=(gram,), moved=half * width * 12)
    return (gram[None], rhs[None], gap.reshape(1, heads, rows_dev))


def solution(mesh):
    in_specs = (
        P("kv", None, "pb", None),
        P("kv", "ctx", None),
        P("kv", "ctx", None),
        P("kv", "ctx"),
    )
    out_specs = (P("kv", ("ctx", "pb"), None), P("kv", ("ctx", "pb"), None), P("kv", None, "pb"))
    return jax.shard_map(shards, mesh=mesh, in_specs=in_specs, out_specs=out_specs, check_vma=False)
```

```python
import functools
import math

import jax
import jax.numpy as jnp
from jax import lax
from jax.experimental import pallas as pl
from jax.experimental.pallas import tpu as pltpu
from jax.sharding import PartitionSpec as P

eps = 1e-06
LOG2E = math.log2(math.e)
F32, BF16 = jnp.float32, jnp.bfloat16
VMEM = pl.BlockSpec(memory_space=pltpu.VMEM)
ANY = pl.BlockSpec(memory_space=pl.ANY)
NT = (((1,), (1,)), ((), ()))
TT = (((0,), (0,)), ((), ()))
STAT = 16


def call(name, body, outs, ins, scratch=(), after=(), flops=0, exps=0, moved=0, limit=20):
    count, skip = len(ins), len(after)

    def ordered(*refs):
        body(*refs[:count], *refs[count + skip :])

    return pl.pallas_call(
        ordered,
        name=name,
        out_shape=[jax.ShapeDtypeStruct(s, d) for s, d in outs],
        in_specs=[VMEM] * count + [ANY] * skip,
        out_specs=[VMEM] * len(outs),
        scratch_shapes=list(scratch),
        compiler_params=pltpu.CompilerParams(vmem_limit_bytes=limit << 20),
        cost_estimate=pl.CostEstimate(flops=flops, transcendentals=exps, bytes_accessed=moved),
    )(*ins, *after)


def split3(x):
    hi = x.astype(BF16)
    rest = x - hi.astype(F32)
    mid = rest.astype(BF16)
    low = (rest - mid.astype(F32)).astype(BF16)
    return hi, mid, low


def joined3(a, b, c):
    return (a.astype(F32) + b.astype(F32)) + c.astype(F32)


def packed3(line):
    hi, mid, low = split3(jnp.broadcast_to(line, (STAT, 128)))
    r = lax.broadcasted_iota(jnp.int32, (STAT, 128), 0)
    return jnp.where(r == 0, hi.astype(F32), jnp.where(r == 1, mid.astype(F32), low.astype(F32))).astype(BF16)


def column(line):
    return jnp.broadcast_to(line, (128, 128)).T


def place(ring):
    at = lax.axis_index("ctx")
    return at // ring, at % ring


def pick_body(sel_ref, keys_ref, out_ref):
    peers, half, width = out_ref.shape
    count = sel_ref.shape[1]
    tokens = keys_ref.shape[0]
    base = lax.axis_index("ctx") * tokens
    first = lax.axis_index("pb") * half
    row = lax.broadcasted_iota(jnp.int32, (half, count), 0) + first
    lane = lax.broadcasted_iota(jnp.int32, (half, count), 1)
    sel = jnp.broadcast_to((sel_ref[...] - base).astype(F32), (half, count))
    col = jnp.sum(jnp.where(row == lane, sel, 0.0), axis=1, keepdims=True).astype(jnp.int32)
    step = 512
    acc = jnp.zeros((half, width), F32)
    for k in range(0, tokens, step):
        at = lax.broadcasted_iota(jnp.int32, (half, step), 1) + k
        hot = (at == col).astype(F32).astype(BF16)
        acc += jnp.dot(hot, keys_ref[k : k + step, :], preferred_element_type=F32)
    mine = acc.astype(BF16)
    for p in range(peers):
        out_ref[p] = mine


def attend(ring, away, q_ref, k_ref, v_ref, s_ref):
    tokens, width = k_ref.shape
    rows = s_ref.shape[1]
    step = 512
    c = LOG2E * width**-0.5
    x, _ = place(ring)
    part = 1 - x if away else x
    q = q_ref[pl.ds(pl.multiple_of(part * rows, rows), rows), :]
    mx = None
    for a in range(0, tokens, step):
        s = lax.dot_general(k_ref[a : a + step, :], q, NT, preferred_element_type=F32)
        s_ref[a : a + step, :] = s
        top = jnp.max(s.reshape(step // 8, 8, rows), axis=0)
        mx = top if mx is None else jnp.maximum(mx, top)
    mc = jnp.max(mx, axis=0, keepdims=True) * c
    total, out = jnp.zeros((8, rows), F32), jnp.zeros((width, rows), F32)
    for a in range(0, tokens, step):
        p = jnp.exp2(s_ref[a : a + step, :] * c - mc)
        total = total + jnp.sum(p.reshape(step // 8, 8, rows), axis=0)
        out = out + lax.dot_general(v_ref[a : a + step, :], p.astype(BF16), TT, preferred_element_type=F32)
    total = jnp.sum(total, axis=0, keepdims=True)
    return (out * (1.0 / total)).T, (mc + jnp.log2(total)) * (1.0 / LOG2E)


def away_body(ring, q_ref, k_ref, v_ref, out_ref, s_ref):
    o, lse = attend(ring, True, q_ref, k_ref, v_ref, s_ref)
    rows = o.shape[0]
    share = rows // ring
    per = 128 // share
    o = o.astype(BF16)
    block = share + STAT
    for g in range(rows // 128):
        three = packed3(lse[:, g * 128 : (g + 1) * 128])
        for j in range(g * per, (g + 1) * per):
            out_ref[j, :share, :] = o[j * share : (j + 1) * share, :]
            out_ref[j, share:block, :] = three


def home_body(ring, q_ref, k_ref, v_ref, out_ref, lse_ref, s_ref):
    o, lse = attend(ring, False, q_ref, k_ref, v_ref, s_ref)
    out_ref[...] = o
    lse_ref[...] = jnp.zeros_like(lse_ref)
    for g in range(o.shape[0] // 128):
        lse_ref[g : g + 1, :] = lse[:, g * 128 : (g + 1) * 128]


def pair_body(o_ref, lse_ref, in_ref, out_ref):
    ring, block, _ = out_ref.shape
    share = block - STAT
    rows = o_ref.shape[0]
    per = 128 // share
    for g in range(rows // 128):
        three = in_ref[g * per, share:block, :].astype(F32)
        other = (three[0:1] + three[1:2]) + three[2:3]
        here = lse_ref[g : g + 1, :]
        top = jnp.maximum(other, here)
        wo, wh = jnp.exp(other - top), jnp.exp(here - top)
        total = wo + wh
        lines = packed3(top + jnp.log(total))
        share_of = column(wh / total)
        for j in range(g * per, (g + 1) * per):
            w = share_of[(j % per) * share : (j % per + 1) * share, :]
            a = in_ref[j, :share, :].astype(F32)
            h = o_ref[j * share : (j + 1) * share, :]
            out_ref[j, :share, :] = (a + w * (h - a)).astype(BF16)
            out_ref[j, share:block, :] = lines


def settle_body(in_ref, out_ref, w_ref):
    ring, block, _ = in_ref.shape
    share = block - STAT
    _, z = place(ring)
    lines = in_ref[:, share:block, :].astype(F32)
    lse = (lines[:, 0, :] + lines[:, 1, :]) + lines[:, 2, :]
    top = jnp.max(lse, axis=0, keepdims=True)
    w = jnp.exp(lse - top)
    total = jnp.sum(w, axis=0, keepdims=True)
    w = w / total
    w_ref[...] = jnp.concatenate([w, jnp.zeros((128 - ring, 128), F32)], axis=0).T
    mine = w_ref[pl.ds(pl.multiple_of((z % (128 // share)) * share, share), share), :]
    acc = jnp.zeros((share, 128), F32)
    for b in range(ring):
        acc = acc + mine[:, b : b + 1] * in_ref[b, :share, :].astype(F32)
    y = (acc * lax.rsqrt(jnp.mean(acc * acc, axis=1, keepdims=True) + eps)).astype(BF16)
    three = packed3(top + jnp.log(total))
    for p in range(ring):
        out_ref[p, :share, :] = y
        out_ref[p, share:, :] = three


def features_body(rt, q_ref, mine_ref, other_ref, own_ref, stat_ref, keep_ref, send_ref, c_ref, f_ref, g_ref):
    rows, width = q_ref.shape
    peers, half, _ = mine_ref.shape
    count = 2 * half
    sel = peers * count
    ring = peers // 2
    c = LOG2E * width**-0.5
    pb = lax.axis_index("pb")
    x, z = place(ring)
    for j in range(peers):
        for ref, core in ((mine_ref, pb), (other_ref, 1 - pb)):
            c_ref[pl.ds(pl.multiple_of(j * count + core * half, half), half), :] = ref[j]
    for t in range(rows // rt):
        s = lax.dot_general(c_ref[...], q_ref[t * rt : (t + 1) * rt, :], NT, preferred_element_type=F32)
        mx = jnp.max(s, axis=0, keepdims=True) * c
        e = jnp.exp2(s * c - mx)
        total = jnp.sum(e, axis=0, keepdims=True)
        f_ref[:, t * rt : (t + 1) * rt] = (e * (sel / total)).astype(BF16)
        stat = (mx + jnp.log2(total)) * (1.0 / LOG2E)
        for g in range(rt // 128):
            r = t * (rt // 128) + g
            stat_ref[r : r + 1, :] = stat[:, g * 128 : (g + 1) * 128]
    there = rows // 2
    lanes = pl.ds(pl.multiple_of(x * there, there), there)
    for k, side in ((0, x), (1, 1 - x)):
        at = pl.multiple_of((side * ring + z) * count, count)
        own_ref[k * count : (k + 1) * count, :] = f_ref[pl.ds(at, count), lanes]
    at = lax.axis_index("ctx") * count
    g_ref[:half, :] = f_ref[pl.ds(pl.multiple_of(at + pb * half, half), half), :]
    g_ref[half:, :] = f_ref[pl.ds(pl.multiple_of(at + (1 - pb) * half, half), half), :]
    step = 512
    for k in range(0, sel, step):
        g = lax.dot_general(g_ref[...], f_ref[k : k + step, :], NT, preferred_element_type=F32)
        g = g * (1.0 / (2 * rows))
        keep_ref[:, k : k + step] = g[:half]
        send_ref[:, k : k + step] = g[half:]


def rhs_body(total_rows, in_ref, own_ref, keep_ref, send_ref, y_ref):
    ring, block, _ = in_ref.shape
    share = block - STAT
    count = keep_ref.shape[0]
    rows = ring * share
    for p in range(ring):
        y_ref[p * share : (p + 1) * share, :] = in_ref[p, :share, :]
    g = jnp.dot(own_ref[...], y_ref[...], preferred_element_type=F32) * (1.0 / total_rows)
    keep_ref[...] = g[:count]
    send_ref[:count, :] = g[count:]
    send_ref[count:, :] = jnp.zeros((8, 128), F32)
    per = 128 // share
    lane = lax.broadcasted_iota(jnp.int32, (1, 128), 1)
    for h in range(rows // 128):
        line = jnp.zeros((1, 128), F32)
        for j in range(per):
            v = in_ref[h * per + j, share:block, :].astype(F32)
            v = (v[0:1] + v[1:2]) + v[2:3]
            line = jnp.where((lane >= j * share) & (lane < (j + 1) * share), v, line)
        send_ref[count + h : count + h + 1, :] = line


def sides_body(ring, keep_ref, sent_ref, got_ref, stat_ref, gsend_ref, mine_ref, out_ref, gap_ref, sum_ref):
    count = keep_ref.shape[0]
    half = count // 2
    sel = gsend_ref.shape[1]
    pb = lax.axis_index("pb")
    x, _ = place(ring)
    sum_ref[...] = keep_ref[...] + got_ref[:count, :]
    mine_ref[...] = sum_ref[pl.ds(pl.multiple_of(pb * half, half), half), :]
    out_ref[:, :sel] = gsend_ref[...]
    out_ref[:, sel:] = sum_ref[pl.ds(pl.multiple_of((1 - pb) * half, half), half), :]
    lines = gap_ref.shape[0] // 2
    here, there = sent_ref[count : count + lines, :], got_ref[count : count + lines, :]
    low = jnp.where(x == 0, here, there)
    high = jnp.where(x == 0, there, here)
    gap_ref[:lines, :] = low - stat_ref[:lines, :]
    gap_ref[lines:, :] = high - stat_ref[lines:, :]


def last_body(g_ref, r_ref, in_ref, gram_ref, rhs_ref):
    sel = g_ref.shape[1]
    gram_ref[...] = g_ref[...] + in_ref[:, :sel]
    rhs_ref[...] = r_ref[...] + in_ref[:, sel:]


def shards(queries, cache_keys, cache_values, sel_index):
    heads, rows_dev, width = queries.shape[1:]
    q = queries[0].reshape(-1, width)
    keys, values = cache_keys[0], cache_values[0]
    rows, tokens = q.shape[0], keys.shape[0]
    blocks = lax.axis_size("ctx")
    ring = blocks // 2
    part = rows // 2
    share = part // ring
    block = share + STAT
    count = sel_index.shape[1]
    half = count // 2
    sel = count * blocks
    total_rows = 2 * rows
    swap = [(0, 1), (1, 0)]
    across = [(i, (i + ring) % blocks) for i in range(blocks)]
    rings = [list(range(ring)), list(range(ring, blocks))]

    def exchange(x):
        return lax.all_to_all(x, "ctx", 0, 0, axis_index_groups=rings, tiled=True)

    (picked,) = call(
        "pick", pick_body, [((blocks, half, width), BF16)], (sel_index, keys), flops=2 * half * tokens * width, moved=tokens * width * 2
    )
    mine = lax.all_to_all(picked, "ctx", 0, 0, tiled=True)
    work = dict(flops=4 * part * tokens * width, exps=part * tokens, moved=tokens * width * 4, scratch=[pltpu.VMEM((tokens, part), F32)])
    (away,) = call(
        "away", functools.partial(away_body, ring), [((ring, block, width), BF16)], (q, keys, values), after=(picked,), **work
    )
    came = lax.ppermute(away, "ctx", across)
    home, lse = call(
        "home",
        functools.partial(home_body, ring),
        [((part, width), F32), ((8, 128), F32)],
        (q, keys, values),
        after=(away,),
        **work,
    )
    (parts,) = call("pair", pair_body, [((ring, block, width), BF16)], (home, lse, came), moved=part * width * 12)
    other = lax.ppermute(mine, "pb", swap)
    (told,) = call(
        "settle",
        settle_body,
        [((ring, block, width), BF16)],
        (exchange(parts),),
        after=(other,),
        scratch=[pltpu.VMEM((128, 128), F32)],
        moved=part * width * 8,
    )
    heard = exchange(told)
    own, stat, gkeep, gsend = call(
        "features",
        functools.partial(features_body, 256),
        [((2 * count, part), BF16), ((rows // 128, 128), F32), ((half, sel), F32), ((half, sel), F32)],
        (q, mine, other),
        after=(told,),
        scratch=[pltpu.VMEM((sel, width), BF16), pltpu.VMEM((sel, rows), BF16), pltpu.VMEM((count, rows), BF16)],
        flops=2 * rows * sel * (width + count),
        exps=rows * sel,
        moved=sel * width * 4,
    )
    rkeep, rsend = call(
        "rhs",
        functools.partial(rhs_body, total_rows),
        [((count, width), F32), ((count + 8, width), F32)],
        (heard, own),
        scratch=[pltpu.VMEM((part, width), BF16)],
        flops=4 * count * part * width,
        moved=part * width * 2,
    )
    rmine, send, gap = call(
        "sides",
        functools.partial(sides_body, ring),
        [((half, width), F32), ((half, sel + width), F32), ((rows // 128, 128), F32)],
        (rkeep, rsend, lax.ppermute(rsend, "ctx", across), stat, gsend),
        scratch=[pltpu.VMEM((count, width), F32)],
        moved=half * sel * 8,
    )
    gram, rhs = call(
        "last",
        last_body,
        [((half, sel), F32), ((half, width), F32)],
        (gkeep, rmine, lax.ppermute(send, "pb", swap)),
        moved=half * sel * 12,
    )
    return (gram[None], rhs[None], gap.reshape(1, heads, rows_dev))


def solution(mesh):
    in_specs = (
        P("kv", None, "pb", None),
        P("kv", "ctx", None),
        P("kv", "ctx", None),
        P("kv", "ctx"),
    )
    out_specs = (P("kv", ("ctx", "pb"), None), P("kv", ("ctx", "pb"), None), P("kv", None, "pb"))
    return jax.shard_map(shards, mesh=mesh, in_specs=in_specs, out_specs=out_specs, check_vma=False)
```

```python
import functools
import math

import jax
import jax.numpy as jnp
from jax import lax
from jax.experimental import pallas as pl
from jax.experimental.pallas import tpu as pltpu
from jax.sharding import PartitionSpec as P

eps = 1e-06
LOG2E = math.log2(math.e)
F32, BF16 = jnp.float32, jnp.bfloat16
VMEM = pl.BlockSpec(memory_space=pltpu.VMEM)
ANY = pl.BlockSpec(memory_space=pl.ANY)
NT = (((1,), (1,)), ((), ()))
TT = (((0,), (0,)), ((), ()))
STAT = 16


def call(name, body, outs, ins, scratch=(), after=(), specs=(), flops=0, exps=0, moved=0, limit=20):
    count, skip = len(ins), len(after)

    def ordered(*refs):
        body(*refs[:count], *refs[count + skip :])

    return pl.pallas_call(
        ordered,
        name=name,
        out_shape=[jax.ShapeDtypeStruct(s, d) for s, d in outs],
        in_specs=(list(specs) or [VMEM] * count) + [ANY] * skip,
        out_specs=[VMEM] * len(outs),
        scratch_shapes=list(scratch),
        compiler_params=pltpu.CompilerParams(vmem_limit_bytes=int(limit * 2**20)),
        cost_estimate=pl.CostEstimate(flops=flops, transcendentals=exps, bytes_accessed=moved),
    )(*ins, *after)


def split3(x):
    hi = x.astype(BF16)
    rest = x - hi.astype(F32)
    mid = rest.astype(BF16)
    low = (rest - mid.astype(F32)).astype(BF16)
    return hi, mid, low


def joined3(a, b, c):
    return (a.astype(F32) + b.astype(F32)) + c.astype(F32)


def packed3(line):
    hi, mid, low = split3(jnp.broadcast_to(line, (STAT, 128)))
    r = lax.broadcasted_iota(jnp.int32, (STAT, 128), 0)
    return jnp.where(r == 0, hi.astype(F32), jnp.where(r == 1, mid.astype(F32), low.astype(F32))).astype(BF16)


def column(line):
    return jnp.broadcast_to(line, (128, 128)).T


def place(ring):
    at = lax.axis_index("ctx")
    return at // ring, at % ring


def attend(ring, away, q_hbm, k_hbm, v_hbm, q_ref, k_ref, v_ref, s_ref, sem):
    rows, width = q_ref.shape
    tokens = k_ref.shape[0]
    step = 512
    c = LOG2E * width**-0.5
    x, _ = place(ring)
    part = 1 - x if away else x
    copies = [pltpu.make_async_copy(q_hbm.at[pl.ds(pl.multiple_of(part * rows, rows), rows)], q_ref, sem.at[0])]
    copies += [pltpu.make_async_copy(k_hbm, k_ref, sem.at[1]), pltpu.make_async_copy(v_hbm, v_ref, sem.at[2])]
    for copy in copies:
        copy.start()
    copies[0].wait()
    copies[1].wait()
    q = q_ref[...]
    mx = None
    for a in range(0, tokens, step):
        s = lax.dot_general(k_ref[a : a + step, :], q, NT, preferred_element_type=F32)
        s_ref[a : a + step, :] = s
        top = jnp.max(s.reshape(step // 8, 8, rows), axis=0)
        mx = top if mx is None else jnp.maximum(mx, top)
    mc = jnp.max(mx, axis=0, keepdims=True) * c
    total, out = jnp.zeros((8, rows), F32), jnp.zeros((width, rows), F32)
    copies[2].wait()
    for a in range(0, tokens, step):
        p = jnp.exp2(s_ref[a : a + step, :] * c - mc)
        total = total + jnp.sum(p.reshape(step // 8, 8, rows), axis=0)
        out = out + lax.dot_general(v_ref[a : a + step, :], p.astype(BF16), TT, preferred_element_type=F32)
    total = jnp.sum(total, axis=0, keepdims=True)
    return (out * (1.0 / total)).T, (mc + jnp.log2(total)) * (1.0 / LOG2E)


def away_body(ring, sel_hbm, q_hbm, k_hbm, v_hbm, out_ref, pick_ref, sel_ref, q_ref, k_ref, v_ref, s_ref, sem, sel_sem):
    fetch = pltpu.make_async_copy(sel_hbm, sel_ref, sel_sem)
    fetch.start()
    o, lse = attend(ring, True, q_hbm, k_hbm, v_hbm, q_ref, k_ref, v_ref, s_ref, sem)
    rows, width = q_ref.shape
    tokens = k_ref.shape[0]
    share = rows // ring
    per = 128 // share
    o = o.astype(BF16)
    block = share + STAT
    for g in range(rows // 128):
        three = packed3(lse[:, g * 128 : (g + 1) * 128])
        for j in range(g * per, (g + 1) * per):
            out_ref[j * block : j * block + share, :] = o[j * share : (j + 1) * share, :]
            out_ref[j * block + share : (j + 1) * block, :] = three
    fetch.wait()
    half = pick_ref.shape[0]
    count = sel_ref.shape[1]
    base = lax.axis_index("ctx") * tokens
    first = lax.axis_index("pb") * half
    row = lax.broadcasted_iota(jnp.int32, (half, count), 0) + first
    lane = lax.broadcasted_iota(jnp.int32, (half, count), 1)
    sel = jnp.broadcast_to((sel_ref[...] - base).astype(F32), (half, count))
    col = jnp.sum(jnp.where(row == lane, sel, 0.0), axis=1, keepdims=True).astype(jnp.int32)
    step = 512
    acc = jnp.zeros((half, width), F32)
    for k in range(0, tokens, step):
        at = lax.broadcasted_iota(jnp.int32, (half, step), 1) + k
        hot = (at == col).astype(F32).astype(BF16)
        acc += jnp.dot(hot, k_ref[k : k + step, :], preferred_element_type=F32)
    mine = acc.astype(BF16)
    pick_ref[...] = mine
    out_ref[ring * block : ring * block + half, :] = mine


def home_body(ring, q_hbm, k_hbm, v_hbm, out_ref, lse_ref, q_ref, k_ref, v_ref, s_ref, sem):
    o, lse = attend(ring, False, q_hbm, k_hbm, v_hbm, q_ref, k_ref, v_ref, s_ref, sem)
    out_ref[...] = o
    lse_ref[...] = jnp.zeros_like(lse_ref)
    for g in range(o.shape[0] // 128):
        lse_ref[g : g + 1, :] = lse[:, g * 128 : (g + 1) * 128]


def pair_body(o_ref, lse_ref, in_ref, pick_ref, out_ref):
    ring = out_ref.shape[0]
    rows = o_ref.shape[0]
    half = pick_ref.shape[0]
    share = rows // ring
    per = 128 // share
    block = share + STAT
    mine, theirs = pick_ref[...], in_ref[ring * block : ring * block + half, :]
    for g in range(rows // 128):
        at = g * per * block
        three = in_ref[at + share : at + block, :].astype(F32)
        other = (three[0:1] + three[1:2]) + three[2:3]
        here = lse_ref[g : g + 1, :]
        top = jnp.maximum(other, here)
        wo, wh = jnp.exp(other - top), jnp.exp(here - top)
        total = wo + wh
        lines = packed3(top + jnp.log(total))
        share_of = column(wh / total)
        for j in range(g * per, (g + 1) * per):
            w = share_of[(j % per) * share : (j % per + 1) * share, :]
            a = in_ref[j * block : j * block + share, :].astype(F32)
            h = o_ref[j * share : (j + 1) * share, :]
            out_ref[j, :share, :] = (a + w * (h - a)).astype(BF16)
            out_ref[j, share:block, :] = lines
            out_ref[j, block : block + half, :] = mine
            out_ref[j, block + half :, :] = theirs


def settle_body(share, in_ref, out_ref, keys_ref, w_ref):
    ring = in_ref.shape[0]
    block = share + STAT
    _, z = place(ring)
    lines = in_ref[:, share:block, :].astype(F32)
    lse = (lines[:, 0, :] + lines[:, 1, :]) + lines[:, 2, :]
    top = jnp.max(lse, axis=0, keepdims=True)
    w = jnp.exp(lse - top)
    total = jnp.sum(w, axis=0, keepdims=True)
    w = w / total
    w_ref[...] = jnp.concatenate([w, jnp.zeros((128 - ring, 128), F32)], axis=0).T
    mine = w_ref[pl.ds(pl.multiple_of((z % (128 // share)) * share, share), share), :]
    acc = jnp.zeros((share, 128), F32)
    for b in range(ring):
        acc = acc + mine[:, b : b + 1] * in_ref[b, :share, :].astype(F32)
    y = (acc * lax.rsqrt(jnp.mean(acc * acc, axis=1, keepdims=True) + eps)).astype(BF16)
    three = packed3(top + jnp.log(total))
    for p in range(ring):
        out_ref[p, :share, :] = y
        out_ref[p, share:, :] = three
        keys_ref[p] = in_ref[p, block:, :]


def features_body(rt, q_ref, mine_ref, other_ref, own_ref, stat_ref, keep_ref, send_ref, c_ref, f_ref, g_ref):
    rows, width = q_ref.shape
    ring, count, _ = mine_ref.shape
    half = count // 2
    sel = 2 * ring * count
    c = LOG2E * width**-0.5
    pb = lax.axis_index("pb")
    x, z = place(ring)
    for j in range(ring):
        for ref, core in ((mine_ref, pb), (other_ref, 1 - pb)):
            for k, side in ((0, x), (1, 1 - x)):
                at = pl.multiple_of((side * ring + j) * count + core * half, half)
                c_ref[pl.ds(at, half), :] = ref[j, k * half : (k + 1) * half, :]
    for t in range(rows // rt):
        s = lax.dot_general(c_ref[...], q_ref[t * rt : (t + 1) * rt, :], NT, preferred_element_type=F32)
        mx = jnp.max(s, axis=0, keepdims=True) * c
        e = jnp.exp2(s * c - mx)
        total = jnp.sum(e, axis=0, keepdims=True)
        f_ref[:, t * rt : (t + 1) * rt] = (e * (sel / total)).astype(BF16)
        stat = (mx + jnp.log2(total)) * (1.0 / LOG2E)
        for g in range(rt // 128):
            r = t * (rt // 128) + g
            stat_ref[r : r + 1, :] = stat[:, g * 128 : (g + 1) * 128]
    there = rows // 2
    lanes = pl.ds(pl.multiple_of(x * there, there), there)
    for k, side in ((0, x), (1, 1 - x)):
        at = pl.multiple_of((side * ring + z) * count, count)
        own_ref[k * count : (k + 1) * count, :] = f_ref[pl.ds(at, count), lanes]
    at = lax.axis_index("ctx") * count
    g_ref[:half, :] = f_ref[pl.ds(pl.multiple_of(at + pb * half, half), half), :]
    g_ref[half:, :] = f_ref[pl.ds(pl.multiple_of(at + (1 - pb) * half, half), half), :]
    step = 512
    for k in range(0, sel, step):
        g = lax.dot_general(g_ref[...], f_ref[k : k + step, :], NT, preferred_element_type=F32)
        g = g * (1.0 / (2 * rows))
        keep_ref[:, k : k + step] = g[:half]
        send_ref[:, k : k + step] = g[half:]


def rhs_body(total_rows, in_ref, own_ref, keep_ref, send_ref, y_ref):
    ring, block, _ = in_ref.shape
    share = block - STAT
    count = keep_ref.shape[0]
    rows = ring * share
    for p in range(ring):
        y_ref[p * share : (p + 1) * share, :] = in_ref[p, :share, :]
    g = jnp.dot(own_ref[...], y_ref[...], preferred_element_type=F32) * (1.0 / total_rows)
    keep_ref[...] = g[:count]
    send_ref[:count, :] = g[count:]
    send_ref[count:, :] = jnp.zeros((8, 128), F32)
    per = 128 // share
    lane = lax.broadcasted_iota(jnp.int32, (1, 128), 1)
    for h in range(rows // 128):
        line = jnp.zeros((1, 128), F32)
        for j in range(per):
            v = in_ref[h * per + j, share:block, :].astype(F32)
            v = (v[0:1] + v[1:2]) + v[2:3]
            line = jnp.where((lane >= j * share) & (lane < (j + 1) * share), v, line)
        send_ref[count + h : count + h + 1, :] = line


def sides_body(ring, keep_ref, sent_ref, got_ref, stat_ref, gsend_ref, mine_ref, out_ref, gap_ref, sum_ref):
    count = keep_ref.shape[0]
    half = count // 2
    sel = gsend_ref.shape[1]
    pb = lax.axis_index("pb")
    x, _ = place(ring)
    sum_ref[...] = keep_ref[...] + got_ref[:count, :]
    mine_ref[...] = sum_ref[pl.ds(pl.multiple_of(pb * half, half), half), :]
    out_ref[:, :sel] = gsend_ref[...]
    out_ref[:, sel:] = sum_ref[pl.ds(pl.multiple_of((1 - pb) * half, half), half), :]
    lines = gap_ref.shape[0] // 2
    here, there = sent_ref[count : count + lines, :], got_ref[count : count + lines, :]
    low = jnp.where(x == 0, here, there)
    high = jnp.where(x == 0, there, here)
    gap_ref[:lines, :] = low - stat_ref[:lines, :]
    gap_ref[lines:, :] = high - stat_ref[lines:, :]


def last_body(g_ref, r_ref, in_ref, gram_ref, rhs_ref):
    sel = g_ref.shape[1]
    gram_ref[...] = g_ref[...] + in_ref[:, :sel]
    rhs_ref[...] = r_ref[...] + in_ref[:, sel:]


def shards(queries, cache_keys, cache_values, sel_index):
    heads, rows_dev, width = queries.shape[1:]
    q = queries[0].reshape(-1, width)
    keys, values = cache_keys[0], cache_values[0]
    rows, tokens = q.shape[0], keys.shape[0]
    blocks = lax.axis_size("ctx")
    ring = blocks // 2
    part = rows // 2
    share = part // ring
    block = share + STAT
    count = sel_index.shape[1]
    half = count // 2
    sel = count * blocks
    total_rows = 2 * rows
    swap = [(0, 1), (1, 0)]
    across = [(i, (i + ring) % blocks) for i in range(blocks)]
    rings = [list(range(ring)), list(range(ring, blocks))]

    def exchange(x):
        return lax.all_to_all(x, "ctx", 0, 0, axis_index_groups=rings, tiled=True)

    held = [
        pltpu.VMEM((part, width), BF16),
        pltpu.VMEM((tokens, width), BF16),
        pltpu.VMEM((tokens, width), BF16),
        pltpu.VMEM((tokens, part), F32),
        pltpu.SemaphoreType.DMA((3,)),
    ]
    work = dict(flops=4 * part * tokens * width, exps=part * tokens, moved=tokens * width * 4, limit=60.0)
    away, picked = call(
        "away",
        functools.partial(away_body, ring),
        [((ring * block + half, width), BF16), ((half, width), BF16)],
        (sel_index, q, keys, values),
        specs=[ANY] * 4,
        scratch=[pltpu.VMEM((1, count), jnp.int32), *held, pltpu.SemaphoreType.DMA],
        **work,
    )
    came = lax.ppermute(away, "ctx", across)
    home, lse = call(
        "home",
        functools.partial(home_body, ring),
        [((part, width), F32), ((8, 128), F32)],
        (q, keys, values),
        specs=[ANY] * 3,
        after=(picked,),
        scratch=held,
        **(work | dict(limit=53.5)),
    )
    (parts,) = call("pair", pair_body, [((ring, block + count, width), BF16)], (home, lse, came, picked), moved=part * width * 12)
    told, mine = call(
        "settle",
        functools.partial(settle_body, share),
        [((ring, block, width), BF16), ((ring, count, width), BF16)],
        (exchange(parts),),
        scratch=[pltpu.VMEM((128, 128), F32)],
        moved=part * width * 8,
    )
    heard = exchange(told)
    other = lax.ppermute(mine, "pb", swap)
    own, stat, gkeep, gsend = call(
        "features",
        functools.partial(features_body, 256),
        [((2 * count, part), BF16), ((rows // 128, 128), F32), ((half, sel), F32), ((half, sel), F32)],
        (q, mine, other),
        after=(told,),
        scratch=[pltpu.VMEM((sel, width), BF16), pltpu.VMEM((sel, rows), BF16), pltpu.VMEM((count, rows), BF16)],
        flops=2 * rows * sel * (width + count),
        exps=rows * sel,
        moved=sel * width * 4,
    )
    rkeep, rsend = call(
        "rhs",
        functools.partial(rhs_body, total_rows),
        [((count, width), F32), ((count + 8, width), F32)],
        (heard, own),
        scratch=[pltpu.VMEM((part, width), BF16)],
        flops=4 * count * part * width,
        moved=part * width * 2,
    )
    rmine, send, gap = call(
        "sides",
        functools.partial(sides_body, ring),
        [((half, width), F32), ((half, sel + width), F32), ((rows // 128, 128), F32)],
        (rkeep, rsend, lax.ppermute(rsend, "ctx", across), stat, gsend),
        scratch=[pltpu.VMEM((count, width), F32)],
        moved=half * sel * 8,
    )
    gram, rhs = call(
        "last",
        last_body,
        [((half, sel), F32), ((half, width), F32)],
        (gkeep, rmine, lax.ppermute(send, "pb", swap)),
        moved=half * sel * 12,
    )
    return (gram[None], rhs[None], gap.reshape(1, heads, rows_dev))


def solution(mesh):
    in_specs = (
        P("kv", None, "pb", None),
        P("kv", "ctx", None),
        P("kv", "ctx", None),
        P("kv", "ctx"),
    )
    out_specs = (P("kv", ("ctx", "pb"), None), P("kv", ("ctx", "pb"), None), P("kv", None, "pb"))
    return jax.shard_map(shards, mesh=mesh, in_specs=in_specs, out_specs=out_specs, check_vma=False)
```

```python
import functools
import math

import jax
import jax.numpy as jnp
from jax import lax
from jax.experimental import pallas as pl
from jax.experimental.pallas import tpu as pltpu
from jax.sharding import PartitionSpec as P

eps = 1e-06
LOG2E = math.log2(math.e)
F32, BF16 = jnp.float32, jnp.bfloat16
VMEM = pl.BlockSpec(memory_space=pltpu.VMEM)
ANY = pl.BlockSpec(memory_space=pl.ANY)
NT = (((1,), (1,)), ((), ()))
TT = (((0,), (0,)), ((), ()))
STAT = 8
FIRST = 12


def call(name, body, outs, ins, scratch=(), after=(), specs=(), flops=0, exps=0, moved=0, limit=20):
    count, skip = len(ins), len(after)

    def ordered(*refs):
        body(*refs[:count], *refs[count + skip :])

    return pl.pallas_call(
        ordered,
        name=name,
        out_shape=[jax.ShapeDtypeStruct(s, d) for s, d in outs],
        in_specs=(list(specs) or [VMEM] * count) + [ANY] * skip,
        out_specs=[VMEM] * len(outs),
        scratch_shapes=list(scratch),
        compiler_params=pltpu.CompilerParams(vmem_limit_bytes=int(limit * 2**20)),
        cost_estimate=pl.CostEstimate(flops=flops, transcendentals=exps, bytes_accessed=moved),
    )(*ins, *after)


def split3(x):
    hi = x.astype(BF16)
    rest = x - hi.astype(F32)
    mid = rest.astype(BF16)
    low = (rest - mid.astype(F32)).astype(BF16)
    return hi, mid, low


def joined3(a, b, c):
    return (a.astype(F32) + b.astype(F32)) + c.astype(F32)


def packed3(line):
    hi, mid, low = split3(jnp.broadcast_to(line, (STAT, 128)))
    r = lax.broadcasted_iota(jnp.int32, (STAT, 128), 0)
    return jnp.where(r == 0, hi.astype(F32), jnp.where(r == 1, mid.astype(F32), low.astype(F32))).astype(BF16)


def column(line):
    return jnp.broadcast_to(line, (128, 128)).T


def slot(z, ring):
    return (z - FIRST) % ring


def place(ring):
    at = lax.axis_index("ctx")
    return at // ring, at % ring


def attend(ring, away, q_hbm, k_hbm, v_hbm, q_ref, k_ref, v_ref, s_ref, sem):
    rows, width = q_ref.shape
    tokens = k_ref.shape[0]
    step = 512
    c = LOG2E * width**-0.5
    x, _ = place(ring)
    part = 1 - x if away else x
    copies = [pltpu.make_async_copy(q_hbm.at[pl.ds(pl.multiple_of(part * rows, rows), rows)], q_ref, sem.at[0])]
    cuts = [pl.ds(0, tokens // 4), pl.ds(tokens // 4, tokens - tokens // 4)]
    copies += [pltpu.make_async_copy(k_hbm.at[cut], k_ref.at[cut], sem.at[1 + n]) for n, cut in enumerate(cuts)]
    copies.append(pltpu.make_async_copy(v_hbm, v_ref, sem.at[3]))
    for copy in copies:
        copy.start()
    copies[0].wait()
    copies[1].wait()
    q = q_ref[...]
    mx = None
    for a in range(0, tokens, step):
        if a == tokens // 4:
            copies[2].wait()
        s = lax.dot_general(k_ref[a : a + step, :], q, NT, preferred_element_type=F32)
        s_ref[a : a + step, :] = s
        top = jnp.max(s.reshape(step // 8, 8, rows), axis=0)
        mx = top if mx is None else jnp.maximum(mx, top)
    mc = jnp.max(mx, axis=0, keepdims=True) * c
    total, out = jnp.zeros((8, rows), F32), jnp.zeros((width, rows), F32)
    copies[3].wait()
    for a in range(0, tokens, step):
        p = jnp.exp2(s_ref[a : a + step, :] * c - mc)
        total = total + jnp.sum(p.reshape(step // 8, 8, rows), axis=0)
        out = out + lax.dot_general(v_ref[a : a + step, :], p.astype(BF16), TT, preferred_element_type=F32)
    total = jnp.sum(total, axis=0, keepdims=True)
    return (out * (1.0 / total)).T, (mc + jnp.log2(total)) * (1.0 / LOG2E)


def away_body(ring, sel_hbm, q_hbm, k_hbm, v_hbm, out_ref, pick_ref, sel_ref, q_ref, k_ref, v_ref, s_ref, sem, sel_sem):
    fetch = pltpu.make_async_copy(sel_hbm, sel_ref, sel_sem)
    fetch.start()
    o, lse = attend(ring, True, q_hbm, k_hbm, v_hbm, q_ref, k_ref, v_ref, s_ref, sem)
    rows, width = q_ref.shape
    tokens = k_ref.shape[0]
    share = rows // ring
    per = 128 // share
    o = o.astype(BF16)
    for g in range(rows // 128):
        three = packed3(lse[:, g * 128 : (g + 1) * 128])
        for j in range(g * per, (g + 1) * per):
            out_ref[j, :share, :] = o[j * share : (j + 1) * share, :]
            out_ref[j, share:, :] = three
    fetch.wait()
    half = pick_ref.shape[0]
    count = sel_ref.shape[1]
    base = lax.axis_index("ctx") * tokens
    first = lax.axis_index("pb") * half
    row = lax.broadcasted_iota(jnp.int32, (half, count), 0) + first
    lane = lax.broadcasted_iota(jnp.int32, (half, count), 1)
    sel = jnp.broadcast_to((sel_ref[...] - base).astype(F32), (half, count))
    col = jnp.sum(jnp.where(row == lane, sel, 0.0), axis=1, keepdims=True).astype(jnp.int32)
    step = 512
    acc = jnp.zeros((half, width), F32)
    for k in range(0, tokens, step):
        at = lax.broadcasted_iota(jnp.int32, (half, step), 1) + k
        hot = (at == col).astype(F32).astype(BF16)
        acc += jnp.dot(hot, k_ref[k : k + step, :], preferred_element_type=F32)
    mine = acc.astype(BF16)
    pick_ref[...] = mine
    out_ref[ring, :half, :] = mine


def home_body(ring, q_hbm, k_hbm, v_hbm, out_ref, lse_ref, q_ref, k_ref, v_ref, s_ref, sem):
    o, lse = attend(ring, False, q_hbm, k_hbm, v_hbm, q_ref, k_ref, v_ref, s_ref, sem)
    out_ref[...] = o
    lse_ref[...] = jnp.zeros_like(lse_ref)
    for g in range(o.shape[0] // 128):
        lse_ref[g : g + 1, :] = lse[:, g * 128 : (g + 1) * 128]


def pair_body(o_ref, lse_ref, in_ref, pick_ref, out_ref):
    ring, length, _ = out_ref.shape
    rows = o_ref.shape[0]
    half = pick_ref.shape[0]
    share = rows // ring
    per = 128 // share
    mine, theirs = pick_ref[...], in_ref[ring, :half, :]
    for g in range(rows // 128):
        three = in_ref[g * per, share:, :].astype(F32)
        other = (three[0:1] + three[1:2]) + three[2:3]
        here = lse_ref[g : g + 1, :]
        top = jnp.maximum(other, here)
        wo, wh = jnp.exp(other - top), jnp.exp(here - top)
        total = wo + wh
        lines = packed3(top + jnp.log(total))
        share_of = column(wh / total)
        for j in range(g * per, (g + 1) * per):
            w = share_of[(j % per) * share : (j % per + 1) * share, :]
            a = in_ref[j, :share, :].astype(F32)
            h = o_ref[j * share : (j + 1) * share, :]
            to = slot(j, ring)
            out_ref[to, :share, :] = (a + w * (h - a)).astype(BF16)
            out_ref[to, share : share + half, :] = mine
            out_ref[to, share + half : length - STAT, :] = theirs
            out_ref[to, length - STAT :, :] = lines


def settle_body(share, in_ref, out_ref, keys_ref, w_ref):
    ring, length, _ = in_ref.shape
    _, z = place(ring)
    lines = in_ref[:, length - STAT :, :].astype(F32)
    lse = (lines[:, 0, :] + lines[:, 1, :]) + lines[:, 2, :]
    top = jnp.max(lse, axis=0, keepdims=True)
    w = jnp.exp(lse - top)
    total = jnp.sum(w, axis=0, keepdims=True)
    w = w / total
    w_ref[...] = jnp.concatenate([w, jnp.zeros((128 - ring, 128), F32)], axis=0).T
    mine = w_ref[pl.ds(pl.multiple_of((z % (128 // share)) * share, share), share), :]
    acc = jnp.zeros((share, 128), F32)
    for b in range(ring):
        acc = acc + mine[:, b : b + 1] * in_ref[b, :share, :].astype(F32)
    y = (acc * lax.rsqrt(jnp.mean(acc * acc, axis=1, keepdims=True) + eps)).astype(BF16)
    three = packed3(top + jnp.log(total))
    for p in range(ring):
        out_ref[p, :share, :] = y
        out_ref[p, share:, :] = three
        keys_ref[p] = in_ref[p, share : length - STAT, :]


def features_body(rt, q_ref, mine_ref, other_ref, own_ref, stat_ref, keep_ref, send_ref, c_ref, f_ref, g_ref):
    rows, width = q_ref.shape
    ring, count, _ = mine_ref.shape
    half = count // 2
    sel = 2 * ring * count
    c = LOG2E * width**-0.5
    pb = lax.axis_index("pb")
    x, z = place(ring)
    for j in range(ring):
        for ref, core in ((mine_ref, pb), (other_ref, 1 - pb)):
            for k, side in ((0, x), (1, 1 - x)):
                at = pl.multiple_of((side * ring + j) * count + core * half, half)
                c_ref[pl.ds(at, half), :] = ref[slot(j, ring), k * half : (k + 1) * half, :]
    for t in range(rows // rt):
        s = lax.dot_general(c_ref[...], q_ref[t * rt : (t + 1) * rt, :], NT, preferred_element_type=F32)
        mx = jnp.max(s, axis=0, keepdims=True) * c
        e = jnp.exp2(s * c - mx)
        total = jnp.sum(e, axis=0, keepdims=True)
        f_ref[:, t * rt : (t + 1) * rt] = (e * (sel / total)).astype(BF16)
        stat = (mx + jnp.log2(total)) * (1.0 / LOG2E)
        for g in range(rt // 128):
            r = t * (rt // 128) + g
            stat_ref[r : r + 1, :] = stat[:, g * 128 : (g + 1) * 128]
    there = rows // 2
    lanes = pl.ds(pl.multiple_of(x * there, there), there)
    for k, side in ((0, x), (1, 1 - x)):
        at = pl.multiple_of((side * ring + z) * count, count)
        own_ref[k * count : (k + 1) * count, :] = f_ref[pl.ds(at, count), lanes]
    at = lax.axis_index("ctx") * count
    g_ref[:half, :] = f_ref[pl.ds(pl.multiple_of(at + pb * half, half), half), :]
    g_ref[half:, :] = f_ref[pl.ds(pl.multiple_of(at + (1 - pb) * half, half), half), :]
    step = 512
    for k in range(0, sel, step):
        g = lax.dot_general(g_ref[...], f_ref[k : k + step, :], NT, preferred_element_type=F32)
        g = g * (1.0 / (2 * rows))
        keep_ref[:, k : k + step] = g[:half]
        send_ref[:, k : k + step] = g[half:]


def rhs_body(total_rows, in_ref, own_ref, keep_ref, send_ref, y_ref):
    ring, block, _ = in_ref.shape
    share = block - STAT
    count = keep_ref.shape[0]
    rows = ring * share
    for p in range(ring):
        y_ref[p * share : (p + 1) * share, :] = in_ref[slot(p, ring), :share, :]
    g = jnp.dot(own_ref[...], y_ref[...], preferred_element_type=F32) * (1.0 / total_rows)
    keep_ref[...] = g[:count]
    send_ref[:count, :] = g[count:]
    send_ref[count:, :] = jnp.zeros((8, 128), F32)
    per = 128 // share
    lane = lax.broadcasted_iota(jnp.int32, (1, 128), 1)
    for h in range(rows // 128):
        line = jnp.zeros((1, 128), F32)
        for j in range(per):
            v = in_ref[slot(h * per + j, ring), share:, :].astype(F32)
            v = (v[0:1] + v[1:2]) + v[2:3]
            line = jnp.where((lane >= j * share) & (lane < (j + 1) * share), v, line)
        send_ref[count + h : count + h + 1, :] = line


def sides_body(ring, keep_ref, sent_ref, got_ref, stat_ref, gsend_ref, mine_ref, out_ref, gap_ref, sum_ref):
    count = keep_ref.shape[0]
    half = count // 2
    sel = gsend_ref.shape[1]
    pb = lax.axis_index("pb")
    x, _ = place(ring)
    sum_ref[...] = keep_ref[...] + got_ref[:count, :]
    mine_ref[...] = sum_ref[pl.ds(pl.multiple_of(pb * half, half), half), :]
    out_ref[:, :sel] = gsend_ref[...]
    out_ref[:, sel:] = sum_ref[pl.ds(pl.multiple_of((1 - pb) * half, half), half), :]
    lines = gap_ref.shape[0] // 2
    here, there = sent_ref[count : count + lines, :], got_ref[count : count + lines, :]
    low = jnp.where(x == 0, here, there)
    high = jnp.where(x == 0, there, here)
    gap_ref[:lines, :] = low - stat_ref[:lines, :]
    gap_ref[lines:, :] = high - stat_ref[lines:, :]


def last_body(g_ref, r_ref, in_ref, gram_ref, rhs_ref):
    sel = g_ref.shape[1]
    gram_ref[...] = g_ref[...] + in_ref[:, :sel]
    rhs_ref[...] = r_ref[...] + in_ref[:, sel:]


def shards(queries, cache_keys, cache_values, sel_index):
    heads, rows_dev, width = queries.shape[1:]
    q = queries[0].reshape(-1, width)
    keys, values = cache_keys[0], cache_values[0]
    rows, tokens = q.shape[0], keys.shape[0]
    blocks = lax.axis_size("ctx")
    ring = blocks // 2
    part = rows // 2
    share = part // ring
    block = share + STAT
    count = sel_index.shape[1]
    half = count // 2
    sel = count * blocks
    total_rows = 2 * rows
    swap = [(0, 1), (1, 0)]
    across = [(i, (i + ring) % blocks) for i in range(blocks)]
    rings = [[side + (j + FIRST) % ring for j in range(ring)] for side in (0, ring)]

    def exchange(x):
        return lax.all_to_all(x, "ctx", 0, 0, axis_index_groups=rings, tiled=True)

    held = [
        pltpu.VMEM((part, width), BF16),
        pltpu.VMEM((tokens, width), BF16),
        pltpu.VMEM((tokens, width), BF16),
        pltpu.VMEM((tokens, part), F32),
        pltpu.SemaphoreType.DMA((4,)),
    ]
    work = dict(flops=4 * part * tokens * width, exps=part * tokens, moved=tokens * width * 4, limit=60.0)
    away, picked = call(
        "away",
        functools.partial(away_body, ring),
        [((ring + 1, block, width), BF16), ((half, width), BF16)],
        (sel_index, q, keys, values),
        specs=[ANY] * 4,
        scratch=[pltpu.VMEM((1, count), jnp.int32), *held, pltpu.SemaphoreType.DMA],
        **work,
    )
    came = lax.ppermute(away, "ctx", across)
    home, lse = call(
        "home",
        functools.partial(home_body, ring),
        [((part, width), F32), ((8, 128), F32)],
        (q, keys, values),
        specs=[ANY] * 3,
        scratch=held,
        **(work | dict(limit=53.5)),
    )
    (parts,) = call("pair", pair_body, [((ring, block + count, width), BF16)], (home, lse, came, picked), moved=part * width * 12)
    told, mine = call(
        "settle",
        functools.partial(settle_body, share),
        [((ring, block, width), BF16), ((ring, count, width), BF16)],
        (exchange(parts),),
        scratch=[pltpu.VMEM((128, 128), F32)],
        moved=part * width * 8,
    )
    heard = exchange(told)
    other = lax.ppermute(mine, "pb", swap)
    own, stat, gkeep, gsend = call(
        "features",
        functools.partial(features_body, 256),
        [((2 * count, part), BF16), ((rows // 128, 128), F32), ((half, sel), F32), ((half, sel), F32)],
        (q, mine, other),
        after=(told,),
        scratch=[pltpu.VMEM((sel, width), BF16), pltpu.VMEM((sel, rows), BF16), pltpu.VMEM((count, rows), BF16)],
        flops=2 * rows * sel * (width + count),
        exps=rows * sel,
        moved=sel * width * 4,
    )
    rkeep, rsend = call(
        "rhs",
        functools.partial(rhs_body, total_rows),
        [((count, width), F32), ((count + 8, width), F32)],
        (heard, own),
        scratch=[pltpu.VMEM((part, width), BF16)],
        flops=4 * count * part * width,
        moved=part * width * 2,
    )
    rmine, send, gap = call(
        "sides",
        functools.partial(sides_body, ring),
        [((half, width), F32), ((half, sel + width), F32), ((rows // 128, 128), F32)],
        (rkeep, rsend, lax.ppermute(rsend, "ctx", across), stat, gsend),
        scratch=[pltpu.VMEM((count, width), F32)],
        moved=half * sel * 8,
    )
    gram, rhs = call(
        "last",
        last_body,
        [((half, sel), F32), ((half, width), F32)],
        (gkeep, rmine, lax.ppermute(send, "pb", swap)),
        moved=half * sel * 12,
    )
    return (gram[None], rhs[None], gap.reshape(1, heads, rows_dev))


def solution(mesh):
    in_specs = (
        P("kv", None, "pb", None),
        P("kv", "ctx", None),
        P("kv", "ctx", None),
        P("kv", "ctx"),
    )
    out_specs = (P("kv", ("ctx", "pb"), None), P("kv", ("ctx", "pb"), None), P("kv", None, "pb"))
    return jax.shard_map(shards, mesh=mesh, in_specs=in_specs, out_specs=out_specs, check_vma=False)
```

```python
import functools
import math

import jax
import jax.numpy as jnp
from jax import lax
from jax.experimental import pallas as pl
from jax.experimental.pallas import tpu as pltpu
from jax.sharding import PartitionSpec as P

eps = 1e-06
LOG2E = math.log2(math.e)
F32, BF16 = jnp.float32, jnp.bfloat16
VMEM = pl.BlockSpec(memory_space=pltpu.VMEM)
ANY = pl.BlockSpec(memory_space=pl.ANY)
NT = (((1,), (1,)), ((), ()))
TT = (((0,), (0,)), ((), ()))
STAT = 8
FIRST = 12


def call(name, body, outs, ins, scratch=(), after=(), specs=(), flops=0, exps=0, moved=0, limit=20):
    count, skip = len(ins), len(after)

    def ordered(*refs):
        body(*refs[:count], *refs[count + skip :])

    return pl.pallas_call(
        ordered,
        name=name,
        out_shape=[jax.ShapeDtypeStruct(s, d) for s, d in outs],
        in_specs=(list(specs) or [VMEM] * count) + [ANY] * skip,
        out_specs=[VMEM] * len(outs),
        scratch_shapes=list(scratch),
        compiler_params=pltpu.CompilerParams(vmem_limit_bytes=int(limit * 2**20)),
        cost_estimate=pl.CostEstimate(flops=flops, transcendentals=exps, bytes_accessed=moved),
    )(*ins, *after)


def split3(x):
    hi = x.astype(BF16)
    rest = x - hi.astype(F32)
    mid = rest.astype(BF16)
    low = (rest - mid.astype(F32)).astype(BF16)
    return hi, mid, low


def joined3(a, b, c):
    return (a.astype(F32) + b.astype(F32)) + c.astype(F32)


def packed3(line):
    hi, mid, low = split3(jnp.broadcast_to(line, (STAT, 128)))
    r = lax.broadcasted_iota(jnp.int32, (STAT, 128), 0)
    return jnp.where(r == 0, hi.astype(F32), jnp.where(r == 1, mid.astype(F32), low.astype(F32))).astype(BF16)


def column(line):
    return jnp.broadcast_to(line, (128, 128)).T


def slot(z, ring):
    return (z - FIRST) % ring


def place(ring):
    at = lax.axis_index("ctx")
    return at // ring, at % ring


def select(sel_ref, k_ref, pick_ref):
    half, width = pick_ref.shape
    count = sel_ref.shape[1]
    tokens = k_ref.shape[0]
    base = lax.axis_index("ctx") * tokens
    first = lax.axis_index("pb") * half
    row = lax.broadcasted_iota(jnp.int32, (half, count), 0) + first
    lane = lax.broadcasted_iota(jnp.int32, (half, count), 1)
    sel = jnp.broadcast_to((sel_ref[...] - base).astype(F32), (half, count))
    col = jnp.sum(jnp.where(row == lane, sel, 0.0), axis=1, keepdims=True).astype(jnp.int32)
    step = 512
    acc = jnp.zeros((half, width), F32)
    for k in range(0, tokens, step):
        at = lax.broadcasted_iota(jnp.int32, (half, step), 1) + k
        hot = (at == col).astype(F32).astype(BF16)
        acc += jnp.dot(hot, k_ref[k : k + step, :], preferred_element_type=F32)
    pick_ref[...] = acc.astype(BF16)


def attend(ring, away, q_hbm, k_hbm, v_hbm, q_ref, k_ref, v_ref, s_ref, sem, fetch=None, pick=None):
    rows, width = q_ref.shape
    tokens = k_ref.shape[0]
    step = 512
    c = LOG2E * width**-0.5
    x, _ = place(ring)
    part = 1 - x if away else x
    copies = [pltpu.make_async_copy(q_hbm.at[pl.ds(pl.multiple_of(part * rows, rows), rows)], q_ref, sem.at[0])]
    cuts = [pl.ds(0, tokens // 4), pl.ds(tokens // 4, tokens - tokens // 4)]
    copies += [pltpu.make_async_copy(k_hbm.at[cut], k_ref.at[cut], sem.at[1 + n]) for n, cut in enumerate(cuts)]
    copies.append(pltpu.make_async_copy(v_hbm, v_ref, sem.at[3]))
    for copy in copies:
        copy.start()
    copies[0].wait()
    copies[1].wait()
    q = q_ref[...]
    mx = None
    for a in range(0, tokens, step):
        if a == tokens // 4:
            copies[2].wait()
            if fetch is not None:
                fetch.wait()
        s = lax.dot_general(k_ref[a : a + step, :], q, NT, preferred_element_type=F32)
        s_ref[a : a + step, :] = s
        top = jnp.max(s.reshape(step // 8, 8, rows), axis=0)
        mx = top if mx is None else jnp.maximum(mx, top)
    mc = jnp.max(mx, axis=0, keepdims=True) * c
    if pick is not None:
        pick()
    total, out = jnp.zeros((8, rows), F32), jnp.zeros((width, rows), F32)
    copies[3].wait()
    for a in range(0, tokens, step):
        p = jnp.exp2(s_ref[a : a + step, :] * c - mc)
        total = total + jnp.sum(p.reshape(step // 8, 8, rows), axis=0)
        out = out + lax.dot_general(v_ref[a : a + step, :], p.astype(BF16), TT, preferred_element_type=F32)
    total = jnp.sum(total, axis=0, keepdims=True)
    return (out * (1.0 / total)).T, (mc + jnp.log2(total)) * (1.0 / LOG2E)


def away_body(ring, sel_hbm, q_hbm, k_hbm, v_hbm, out_ref, pick_ref, sel_ref, q_ref, k_ref, v_ref, s_ref, sem, sel_sem):
    fetch = pltpu.make_async_copy(sel_hbm, sel_ref, sel_sem)
    fetch.start()

    def pick():
        select(sel_ref, k_ref, pick_ref)
        out_ref[ring, : pick_ref.shape[0], :] = pick_ref[...]

    o, lse = attend(ring, True, q_hbm, k_hbm, v_hbm, q_ref, k_ref, v_ref, s_ref, sem, fetch, pick)
    rows = q_ref.shape[0]
    share = rows // ring
    per = 128 // share
    o = o.astype(BF16)
    for g in range(rows // 128):
        three = packed3(lse[:, g * 128 : (g + 1) * 128])
        for j in range(g * per, (g + 1) * per):
            out_ref[j, :share, :] = o[j * share : (j + 1) * share, :]
            out_ref[j, share:, :] = three


def home_body(ring, q_hbm, k_hbm, v_hbm, out_ref, lse_ref, q_ref, k_ref, v_ref, s_ref, sem):
    o, lse = attend(ring, False, q_hbm, k_hbm, v_hbm, q_ref, k_ref, v_ref, s_ref, sem)
    out_ref[...] = o
    lse_ref[...] = jnp.zeros_like(lse_ref)
    for g in range(o.shape[0] // 128):
        lse_ref[g : g + 1, :] = lse[:, g * 128 : (g + 1) * 128]


def pair_body(o_ref, lse_ref, in_ref, pick_ref, out_ref):
    ring, length, _ = out_ref.shape
    rows = o_ref.shape[0]
    half = pick_ref.shape[0]
    share = rows // ring
    per = 128 // share
    mine, theirs = pick_ref[...], in_ref[ring, :half, :]
    for g in range(rows // 128):
        three = in_ref[g * per, share:, :].astype(F32)
        other = (three[0:1] + three[1:2]) + three[2:3]
        here = lse_ref[g : g + 1, :]
        top = jnp.maximum(other, here)
        wo, wh = jnp.exp(other - top), jnp.exp(here - top)
        total = wo + wh
        lines = packed3(top + jnp.log(total))
        share_of = column(wh / total)
        for j in range(g * per, (g + 1) * per):
            w = share_of[(j % per) * share : (j % per + 1) * share, :]
            a = in_ref[j, :share, :].astype(F32)
            h = o_ref[j * share : (j + 1) * share, :]
            to = slot(j, ring)
            out_ref[to, :share, :] = (a + w * (h - a)).astype(BF16)
            out_ref[to, share : share + half, :] = mine
            out_ref[to, share + half : length - STAT, :] = theirs
            out_ref[to, length - STAT :, :] = lines


def settle_body(share, in_ref, out_ref, keys_ref, w_ref):
    ring, length, _ = in_ref.shape
    _, z = place(ring)
    lines = in_ref[:, length - STAT :, :].astype(F32)
    lse = (lines[:, 0, :] + lines[:, 1, :]) + lines[:, 2, :]
    top = jnp.max(lse, axis=0, keepdims=True)
    w = jnp.exp(lse - top)
    total = jnp.sum(w, axis=0, keepdims=True)
    w = w / total
    w_ref[...] = jnp.concatenate([w, jnp.zeros((128 - ring, 128), F32)], axis=0).T
    mine = w_ref[pl.ds(pl.multiple_of((z % (128 // share)) * share, share), share), :]
    acc = jnp.zeros((share, 128), F32)
    for b in range(ring):
        acc = acc + mine[:, b : b + 1] * in_ref[b, :share, :].astype(F32)
    y = (acc * lax.rsqrt(jnp.mean(acc * acc, axis=1, keepdims=True) + eps)).astype(BF16)
    three = packed3(top + jnp.log(total))
    for p in range(ring):
        out_ref[p, :share, :] = y
        out_ref[p, share:, :] = three
        keys_ref[p] = in_ref[p, share : length - STAT, :]


def features_body(rt, q_ref, mine_ref, other_ref, own_ref, stat_ref, keep_ref, send_ref, c_ref, f_ref, g_ref):
    rows, width = q_ref.shape
    ring, count, _ = mine_ref.shape
    half = count // 2
    sel = 2 * ring * count
    c = LOG2E * width**-0.5
    pb = lax.axis_index("pb")
    x, z = place(ring)
    for j in range(ring):
        for ref, core in ((mine_ref, pb), (other_ref, 1 - pb)):
            for k, side in ((0, x), (1, 1 - x)):
                at = pl.multiple_of((side * ring + j) * count + core * half, half)
                c_ref[pl.ds(at, half), :] = ref[slot(j, ring), k * half : (k + 1) * half, :]
    for t in range(rows // rt):
        s = lax.dot_general(c_ref[...], q_ref[t * rt : (t + 1) * rt, :], NT, preferred_element_type=F32)
        mx = jnp.max(s, axis=0, keepdims=True) * c
        e = jnp.exp2(s * c - mx)
        total = jnp.sum(e, axis=0, keepdims=True)
        f_ref[:, t * rt : (t + 1) * rt] = (e * (sel / total)).astype(BF16)
        stat = (mx + jnp.log2(total)) * (1.0 / LOG2E)
        for g in range(rt // 128):
            r = t * (rt // 128) + g
            stat_ref[r : r + 1, :] = stat[:, g * 128 : (g + 1) * 128]
    there = rows // 2
    lanes = pl.ds(pl.multiple_of(x * there, there), there)
    for k, side in ((0, x), (1, 1 - x)):
        at = pl.multiple_of((side * ring + z) * count, count)
        own_ref[k * count : (k + 1) * count, :] = f_ref[pl.ds(at, count), lanes]
    at = lax.axis_index("ctx") * count
    g_ref[:half, :] = f_ref[pl.ds(pl.multiple_of(at + pb * half, half), half), :]
    g_ref[half:, :] = f_ref[pl.ds(pl.multiple_of(at + (1 - pb) * half, half), half), :]
    step = 512
    for k in range(0, sel, step):
        g = lax.dot_general(g_ref[...], f_ref[k : k + step, :], NT, preferred_element_type=F32)
        g = g * (1.0 / (2 * rows))
        keep_ref[:, k : k + step] = g[:half]
        send_ref[:, k : k + step] = g[half:]


def rhs_body(total_rows, in_ref, own_ref, send_ref, y_ref, g_ref):
    ring, block, _ = in_ref.shape
    share = block - STAT
    half = send_ref.shape[1] - 8
    rows = ring * share
    x, _ = place(ring)
    for p in range(ring):
        y_ref[p * share : (p + 1) * share, :] = in_ref[slot(p, ring), :share, :]
    g_ref[...] = jnp.dot(own_ref[...], y_ref[...], preferred_element_type=F32) * (1.0 / total_rows)
    per = 128 // share
    lane = lax.broadcasted_iota(jnp.int32, (1, 128), 1)
    lines = []
    for h in range(rows // 128):
        line = jnp.zeros((1, 128), F32)
        for j in range(per):
            v = in_ref[slot(h * per + j, ring), share:, :].astype(F32)
            v = (v[0:1] + v[1:2]) + v[2:3]
            line = jnp.where((lane >= j * share) & (lane < (j + 1) * share), v, line)
        lines.append(line)
    lines = jnp.concatenate(lines + [jnp.zeros((8 - len(lines), 128), F32)], axis=0)
    for k in range(4):
        other = x if k < 2 else 1 - x
        send_ref[k, :half, :] = g_ref[pl.ds(pl.multiple_of(other * (2 * half) + (k % 2) * half, half), half), :]
        send_ref[k, half:, :] = lines


def last_body(got_ref, stat_ref, keep_ref, in_ref, gram_ref, rhs_ref, gap_ref):
    half = rhs_ref.shape[0]
    rhs_ref[...] = (got_ref[0, :half, :] + got_ref[1, :half, :]) + (got_ref[2, :half, :] + got_ref[3, :half, :])
    gram_ref[...] = keep_ref[...] + in_ref[...]
    pb = lax.axis_index("pb")
    lines = gap_ref.shape[0] // 2
    gap_ref[:lines, :] = got_ref[pb, half : half + lines, :] - stat_ref[:lines, :]
    gap_ref[lines:, :] = got_ref[2 + pb, half : half + lines, :] - stat_ref[lines:, :]


def shards(queries, cache_keys, cache_values, sel_index):
    heads, rows_dev, width = queries.shape[1:]
    q = queries[0].reshape(-1, width)
    keys, values = cache_keys[0], cache_values[0]
    rows, tokens = q.shape[0], keys.shape[0]
    blocks = lax.axis_size("ctx")
    ring = blocks // 2
    part = rows // 2
    share = part // ring
    block = share + STAT
    count = sel_index.shape[1]
    half = count // 2
    sel = count * blocks
    total_rows = 2 * rows
    swap = [(0, 1), (1, 0)]
    across = [(i, (i + ring) % blocks) for i in range(blocks)]
    rings = [[side + (j + FIRST) % ring for j in range(ring)] for side in (0, ring)]

    def exchange(x):
        return lax.all_to_all(x, "ctx", 0, 0, axis_index_groups=rings, tiled=True)

    held = [
        pltpu.VMEM((part, width), BF16),
        pltpu.VMEM((tokens, width), BF16),
        pltpu.VMEM((tokens, width), BF16),
        pltpu.VMEM((tokens, part), F32),
        pltpu.SemaphoreType.DMA((4,)),
    ]
    work = dict(flops=4 * part * tokens * width, exps=part * tokens, moved=tokens * width * 4, limit=60.0)
    away, picked = call(
        "away",
        functools.partial(away_body, ring),
        [((ring + 1, block, width), BF16), ((half, width), BF16)],
        (sel_index, q, keys, values),
        specs=[ANY] * 4,
        scratch=[pltpu.VMEM((1, count), jnp.int32), *held, pltpu.SemaphoreType.DMA],
        **work,
    )
    came = lax.ppermute(away, "ctx", across)
    home, lse = call(
        "home",
        functools.partial(home_body, ring),
        [((part, width), F32), ((8, 128), F32)],
        (q, keys, values),
        specs=[ANY] * 3,
        scratch=held,
        **(work | dict(limit=53.5)),
    )
    (parts,) = call("pair", pair_body, [((ring, block + count, width), BF16)], (home, lse, came, picked), moved=part * width * 12)
    told, mine = call(
        "settle",
        functools.partial(settle_body, share),
        [((ring, block, width), BF16), ((ring, count, width), BF16)],
        (exchange(parts),),
        scratch=[pltpu.VMEM((128, 128), F32)],
        moved=part * width * 8,
    )
    heard = exchange(told)
    other = lax.ppermute(mine, "pb", swap)
    own, stat, gkeep, gsend = call(
        "features",
        functools.partial(features_body, 256),
        [((2 * count, part), BF16), ((rows // 128, 128), F32), ((half, sel), F32), ((half, sel), F32)],
        (q, mine, other),
        after=(told,),
        scratch=[pltpu.VMEM((sel, width), BF16), pltpu.VMEM((sel, rows), BF16), pltpu.VMEM((count, rows), BF16)],
        flops=2 * rows * sel * (width + count),
        exps=rows * sel,
        moved=sel * width * 4,
    )
    quads = [[2 * (side + z) + core for side in (0, ring) for core in (0, 1)] for z in range(ring)]
    (send,) = call(
        "rhs",
        functools.partial(rhs_body, total_rows),
        [((4, half + 8, width), F32)],
        (heard, own),
        scratch=[pltpu.VMEM((part, width), BF16), pltpu.VMEM((2 * count, width), F32)],
        flops=4 * count * part * width,
        moved=part * width * 2,
    )
    got = lax.all_to_all(send, ("ctx", "pb"), 0, 0, axis_index_groups=quads, tiled=True)
    gram, rhs, gap = call(
        "last",
        last_body,
        [((half, sel), F32), ((half, width), F32), ((rows // 128, 128), F32)],
        (got, stat, gkeep, lax.ppermute(gsend, "pb", swap)),
        moved=half * sel * 12,
    )
    return (gram[None], rhs[None], gap.reshape(1, heads, rows_dev))


def solution(mesh):
    in_specs = (
        P("kv", None, "pb", None),
        P("kv", "ctx", None),
        P("kv", "ctx", None),
        P("kv", "ctx"),
    )
    out_specs = (P("kv", ("ctx", "pb"), None), P("kv", ("ctx", "pb"), None), P("kv", None, "pb"))
    return jax.shard_map(shards, mesh=mesh, in_specs=in_specs, out_specs=out_specs, check_vma=False)
```

```python
import functools
import math

import jax
import jax.numpy as jnp
from jax import lax
from jax.experimental import pallas as pl
from jax.experimental.pallas import tpu as pltpu
from jax.sharding import PartitionSpec as P

eps = 1e-06
LOG2E = math.log2(math.e)
F32, F16, BF16 = jnp.float32, jnp.float16, jnp.bfloat16
VMEM = pl.BlockSpec(memory_space=pltpu.VMEM)
ANY = pl.BlockSpec(memory_space=pl.ANY)
NT = (((1,), (1,)), ((), ()))
TT = (((0,), (0,)), ((), ()))
STAT = 8
FIRST = 12


def call(name, body, outs, ins, scratch=(), after=(), specs=(), flops=0, exps=0, moved=0, limit=20):
    count, skip = len(ins), len(after)

    def ordered(*refs):
        body(*refs[:count], *refs[count + skip :])

    return pl.pallas_call(
        ordered,
        name=name,
        out_shape=[jax.ShapeDtypeStruct(s, d) for s, d in outs],
        in_specs=(list(specs) or [VMEM] * count) + [ANY] * skip,
        out_specs=[VMEM] * len(outs),
        scratch_shapes=list(scratch),
        compiler_params=pltpu.CompilerParams(vmem_limit_bytes=int(limit * 2**20)),
        cost_estimate=pl.CostEstimate(flops=flops, transcendentals=exps, bytes_accessed=moved),
    )(*ins, *after)


def split3(x):
    hi = x.astype(BF16)
    rest = x - hi.astype(F32)
    mid = rest.astype(BF16)
    low = (rest - mid.astype(F32)).astype(BF16)
    return hi, mid, low


def joined3(a, b, c):
    return (a.astype(F32) + b.astype(F32)) + c.astype(F32)


def packed3(line):
    hi, mid, low = split3(jnp.broadcast_to(line, (STAT, 128)))
    r = lax.broadcasted_iota(jnp.int32, (STAT, 128), 0)
    return jnp.where(r == 0, hi.astype(F32), jnp.where(r == 1, mid.astype(F32), low.astype(F32))).astype(BF16)


def column(line):
    return jnp.broadcast_to(line, (128, 128)).T


def slot(z, ring):
    return (z - FIRST) % ring


def place(ring):
    at = lax.axis_index("ctx")
    return at // ring, at % ring


def select(sel_ref, k_ref, pick_ref):
    half, width = pick_ref.shape
    count = sel_ref.shape[1]
    tokens = k_ref.shape[0]
    base = lax.axis_index("ctx") * tokens
    first = lax.axis_index("pb") * half
    row = lax.broadcasted_iota(jnp.int32, (half, count), 0) + first
    lane = lax.broadcasted_iota(jnp.int32, (half, count), 1)
    sel = jnp.broadcast_to((sel_ref[...] - base).astype(F32), (half, count))
    col = jnp.sum(jnp.where(row == lane, sel, 0.0), axis=1, keepdims=True).astype(jnp.int32)
    step = 512
    acc = jnp.zeros((half, width), F32)
    for k in range(0, tokens, step):
        at = lax.broadcasted_iota(jnp.int32, (half, step), 1) + k
        hot = (at == col).astype(F32).astype(BF16)
        acc += jnp.dot(hot, k_ref[k : k + step, :], preferred_element_type=F32)
    pick_ref[...] = acc


def attend(ring, away, q_hbm, k_hbm, v_hbm, q_ref, k_ref, v_ref, s_ref, sem, fetch=None, pick=None):
    rows, width = q_ref.shape
    tokens = k_ref.shape[0]
    step = 512
    c = LOG2E * width**-0.5
    x, _ = place(ring)
    part = 1 - x if away else x
    copies = [pltpu.make_async_copy(q_hbm.at[pl.ds(pl.multiple_of(part * rows, rows), rows)], q_ref, sem.at[0])]
    cuts = [pl.ds(0, tokens // 4), pl.ds(tokens // 4, tokens - tokens // 4)]
    copies += [pltpu.make_async_copy(k_hbm.at[cut], k_ref.at[cut], sem.at[1 + n]) for n, cut in enumerate(cuts)]
    copies.append(pltpu.make_async_copy(v_hbm, v_ref, sem.at[3]))
    for copy in copies:
        copy.start()
    copies[0].wait()
    copies[1].wait()
    q = q_ref[...]
    mx = None
    for a in range(0, tokens, step):
        if a == tokens // 4:
            copies[2].wait()
            if fetch is not None:
                fetch.wait()
        s = lax.dot_general(k_ref[a : a + step, :], q, NT, preferred_element_type=F32)
        s_ref[a : a + step, :] = s
        top = jnp.max(s.reshape(step // 8, 8, rows), axis=0)
        mx = top if mx is None else jnp.maximum(mx, top)
    mc = jnp.max(mx, axis=0, keepdims=True) * c
    if pick is not None:
        pick()
    total, out = jnp.zeros((8, rows), F32), jnp.zeros((width, rows), F32)
    copies[3].wait()
    for a in range(0, tokens, step):
        p = jnp.exp2(s_ref[a : a + step, :] * c - mc)
        total = total + jnp.sum(p.reshape(step // 8, 8, rows), axis=0)
        out = out + lax.dot_general(v_ref[a : a + step, :], p.astype(BF16), TT, preferred_element_type=F32)
    total = jnp.sum(total, axis=0, keepdims=True)
    return (out * (1.0 / total)).T, (mc + jnp.log2(total)) * (1.0 / LOG2E)


def away_body(ring, sel_hbm, q_hbm, k_hbm, v_hbm, out_ref, pick_ref, sel_ref, q_ref, k_ref, v_ref, s_ref, sem, sel_sem):
    fetch = pltpu.make_async_copy(sel_hbm, sel_ref, sel_sem)
    fetch.start()

    def pick():
        select(sel_ref, k_ref, pick_ref)
        out_ref[ring, : pick_ref.shape[0], :] = pick_ref[...]

    o, lse = attend(ring, True, q_hbm, k_hbm, v_hbm, q_ref, k_ref, v_ref, s_ref, sem, fetch, pick)
    rows = q_ref.shape[0]
    share = rows // ring
    per = 128 // share
    for g in range(rows // 128):
        line = jnp.broadcast_to(lse[:, g * 128 : (g + 1) * 128], (STAT, 128))
        for j in range(g * per, (g + 1) * per):
            out_ref[j, :share, :] = o[j * share : (j + 1) * share, :]
            out_ref[j, share:, :] = line


def home_body(ring, q_hbm, k_hbm, v_hbm, out_ref, lse_ref, q_ref, k_ref, v_ref, s_ref, sem):
    o, lse = attend(ring, False, q_hbm, k_hbm, v_hbm, q_ref, k_ref, v_ref, s_ref, sem)
    out_ref[...] = o
    lse_ref[...] = jnp.zeros_like(lse_ref)
    for g in range(o.shape[0] // 128):
        lse_ref[g : g + 1, :] = lse[:, g * 128 : (g + 1) * 128]


def pair_body(o_ref, lse_ref, in_ref, pick_ref, out_ref):
    ring, length, _ = out_ref.shape
    rows = o_ref.shape[0]
    half = pick_ref.shape[0]
    share = rows // ring
    per = 128 // share
    mine, theirs = pick_ref[...], in_ref[ring, :half, :]
    for g in range(rows // 128):
        other = in_ref[g * per, share : share + 1, :]
        here = lse_ref[g : g + 1, :]
        top = jnp.maximum(other, here)
        wo, wh = jnp.exp(other - top), jnp.exp(here - top)
        total = wo + wh
        lines = packed3(top + jnp.log(total))
        share_of = column(wh / total)
        for j in range(g * per, (g + 1) * per):
            w = share_of[(j % per) * share : (j % per + 1) * share, :]
            a = in_ref[j, :share, :]
            h = o_ref[j * share : (j + 1) * share, :]
            to = slot(j, ring)
            out_ref[to, :share, :] = a + w * (h - a)
            out_ref[to, share : share + half, :] = mine
            out_ref[to, share + half : length - STAT, :] = theirs
            out_ref[to, length - STAT :, :] = lines.astype(F32)


def settle_body(share, in_ref, out_ref, keys_ref, w_ref):
    ring, length, _ = in_ref.shape
    _, z = place(ring)
    lines = in_ref[:, length - STAT :, :]
    lse = (lines[:, 0, :] + lines[:, 1, :]) + lines[:, 2, :]
    top = jnp.max(lse, axis=0, keepdims=True)
    w = jnp.exp(lse - top)
    total = jnp.sum(w, axis=0, keepdims=True)
    w = w / total
    w_ref[...] = jnp.concatenate([w, jnp.zeros((128 - ring, 128), F32)], axis=0).T
    mine = w_ref[pl.ds(pl.multiple_of((z % (128 // share)) * share, share), share), :]
    acc = jnp.zeros((share, 128), F32)
    for b in range(ring):
        acc = acc + mine[:, b : b + 1] * in_ref[b, :share, :]
    y = (acc * lax.rsqrt(jnp.mean(acc * acc, axis=1, keepdims=True) + eps)).astype(BF16)
    three = packed3(top + jnp.log(total))
    for p in range(ring):
        out_ref[p, :share, :] = y
        out_ref[p, share:, :] = three
        keys_ref[p] = in_ref[p, share : length - STAT, :].astype(BF16)


def features_body(rt, q_ref, mine_ref, other_ref, own_ref, stat_ref, keep_ref, send_ref, c_ref, f_ref, g_ref):
    rows, width = q_ref.shape
    ring, count, _ = mine_ref.shape
    half = count // 2
    sel = 2 * ring * count
    c = LOG2E * width**-0.5
    pb = lax.axis_index("pb")
    x, z = place(ring)
    for j in range(ring):
        for ref, core in ((mine_ref, pb), (other_ref, 1 - pb)):
            for k, side in ((0, x), (1, 1 - x)):
                at = pl.multiple_of((side * ring + j) * count + core * half, half)
                c_ref[pl.ds(at, half), :] = ref[slot(j, ring), k * half : (k + 1) * half, :]
    for t in range(rows // rt):
        s = lax.dot_general(c_ref[...], q_ref[t * rt : (t + 1) * rt, :], NT, preferred_element_type=F32)
        mx = jnp.max(s, axis=0, keepdims=True) * c
        e = jnp.exp2(s * c - mx)
        total = jnp.sum(e, axis=0, keepdims=True)
        f_ref[:, t * rt : (t + 1) * rt] = (e * (sel / total)).astype(BF16)
        stat = (mx + jnp.log2(total)) * (1.0 / LOG2E)
        for g in range(rt // 128):
            r = t * (rt // 128) + g
            stat_ref[r : r + 1, :] = stat[:, g * 128 : (g + 1) * 128]
    there = rows // 2
    lanes = pl.ds(pl.multiple_of(x * there, there), there)
    for k, side in ((0, x), (1, 1 - x)):
        at = pl.multiple_of((side * ring + z) * count, count)
        own_ref[k * count : (k + 1) * count, :] = f_ref[pl.ds(at, count), lanes]
    at = lax.axis_index("ctx") * count
    g_ref[:half, :] = f_ref[pl.ds(pl.multiple_of(at + pb * half, half), half), :]
    g_ref[half:, :] = f_ref[pl.ds(pl.multiple_of(at + (1 - pb) * half, half), half), :]
    step = 512
    for k in range(0, sel, step):
        g = lax.dot_general(g_ref[...], f_ref[k : k + step, :], NT, preferred_element_type=F32)
        g = g * (1.0 / (2 * rows))
        keep_ref[:, k : k + step] = g[:half]
        send_ref[:, k : k + step] = g[half:]


def rhs_body(total_rows, in_ref, own_ref, send_ref, y_ref, g_ref):
    ring, block, _ = in_ref.shape
    share = block - STAT
    half = send_ref.shape[1] - 8
    rows = ring * share
    x, _ = place(ring)
    for p in range(ring):
        y_ref[p * share : (p + 1) * share, :] = in_ref[slot(p, ring), :share, :]
    g_ref[...] = jnp.dot(own_ref[...], y_ref[...], preferred_element_type=F32) * (1.0 / total_rows)
    per = 128 // share
    lane = lax.broadcasted_iota(jnp.int32, (1, 128), 1)
    lines = []
    for h in range(rows // 128):
        line = jnp.zeros((1, 128), F32)
        for j in range(per):
            v = in_ref[slot(h * per + j, ring), share:, :].astype(F32)
            v = (v[0:1] + v[1:2]) + v[2:3]
            line = jnp.where((lane >= j * share) & (lane < (j + 1) * share), v, line)
        lines.append(line)
    lines = jnp.concatenate(lines + [jnp.zeros((8 - len(lines), 128), F32)], axis=0)
    for k in range(4):
        other = x if k < 2 else 1 - x
        send_ref[k, :half, :] = g_ref[pl.ds(pl.multiple_of(other * (2 * half) + (k % 2) * half, half), half), :]
        send_ref[k, half:, :] = lines


def last_body(got_ref, stat_ref, keep_ref, in_ref, gram_ref, rhs_ref, gap_ref):
    half = rhs_ref.shape[0]
    rhs_ref[...] = (got_ref[0, :half, :] + got_ref[1, :half, :]) + (got_ref[2, :half, :] + got_ref[3, :half, :])
    gram_ref[...] = keep_ref[...] + in_ref[...]
    pb = lax.axis_index("pb")
    lines = gap_ref.shape[0] // 2
    gap_ref[:lines, :] = got_ref[pb, half : half + lines, :] - stat_ref[:lines, :]
    gap_ref[lines:, :] = got_ref[2 + pb, half : half + lines, :] - stat_ref[lines:, :]


def shards(queries, cache_keys, cache_values, sel_index):
    heads, rows_dev, width = queries.shape[1:]
    q = queries[0].reshape(-1, width)
    keys, values = cache_keys[0], cache_values[0]
    rows, tokens = q.shape[0], keys.shape[0]
    blocks = lax.axis_size("ctx")
    ring = blocks // 2
    part = rows // 2
    share = part // ring
    block = share + STAT
    count = sel_index.shape[1]
    half = count // 2
    sel = count * blocks
    total_rows = 2 * rows
    swap = [(0, 1), (1, 0)]
    across = [(i, (i + ring) % blocks) for i in range(blocks)]
    rings = [[side + (j + FIRST) % ring for j in range(ring)] for side in (0, ring)]

    def exchange(x):
        return lax.all_to_all(x, "ctx", 0, 0, axis_index_groups=rings, tiled=True)

    held = [
        pltpu.VMEM((part, width), BF16),
        pltpu.VMEM((tokens, width), BF16),
        pltpu.VMEM((tokens, width), BF16),
        pltpu.VMEM((tokens, part), F32),
        pltpu.SemaphoreType.DMA((4,)),
    ]
    work = dict(flops=4 * part * tokens * width, exps=part * tokens, moved=tokens * width * 4, limit=60.0)
    away, picked = call(
        "away",
        functools.partial(away_body, ring),
        [((ring + 1, block, width), F32), ((half, width), F32)],
        (sel_index, q, keys, values),
        specs=[ANY] * 4,
        scratch=[pltpu.VMEM((1, count), jnp.int32), *held, pltpu.SemaphoreType.DMA],
        **work,
    )
    came = lax.ppermute(away, "ctx", across)
    home, lse = call(
        "home",
        functools.partial(home_body, ring),
        [((part, width), F32), ((8, 128), F32)],
        (q, keys, values),
        specs=[ANY] * 3,
        scratch=held,
        **(work | dict(limit=53.5)),
    )
    (parts,) = call("pair", pair_body, [((ring, block + count, width), F32)], (home, lse, came, picked), moved=part * width * 12)
    told, mine = call(
        "settle",
        functools.partial(settle_body, share),
        [((ring, block, width), BF16), ((ring, count, width), BF16)],
        (exchange(parts.astype(F16)).astype(F32),),
        scratch=[pltpu.VMEM((128, 128), F32)],
        moved=part * width * 8,
    )
    heard = exchange(told)
    other = lax.ppermute(mine, "pb", swap)
    own, stat, gkeep, gsend = call(
        "features",
        functools.partial(features_body, 256),
        [((2 * count, part), BF16), ((rows // 128, 128), F32), ((half, sel), F32), ((half, sel), F32)],
        (q, mine, other),
        after=(told,),
        scratch=[pltpu.VMEM((sel, width), BF16), pltpu.VMEM((sel, rows), BF16), pltpu.VMEM((count, rows), BF16)],
        flops=2 * rows * sel * (width + count),
        exps=rows * sel,
        moved=sel * width * 4,
    )
    quads = [[2 * (side + z) + core for side in (0, ring) for core in (0, 1)] for z in range(ring)]
    (send,) = call(
        "rhs",
        functools.partial(rhs_body, total_rows),
        [((4, half + 8, width), F32)],
        (heard, own),
        scratch=[pltpu.VMEM((part, width), BF16), pltpu.VMEM((2 * count, width), F32)],
        flops=4 * count * part * width,
        moved=part * width * 2,
    )
    got = lax.all_to_all(send, ("ctx", "pb"), 0, 0, axis_index_groups=quads, tiled=True)
    gram, rhs, gap = call(
        "last",
        last_body,
        [((half, sel), F32), ((half, width), F32), ((rows // 128, 128), F32)],
        (got, stat, gkeep, lax.ppermute(gsend, "pb", swap)),
        moved=half * sel * 12,
    )
    return (gram[None], rhs[None], gap.reshape(1, heads, rows_dev))


def solution(mesh):
    in_specs = (
        P("kv", None, "pb", None),
        P("kv", "ctx", None),
        P("kv", "ctx", None),
        P("kv", "ctx"),
    )
    out_specs = (P("kv", ("ctx", "pb"), None), P("kv", ("ctx", "pb"), None), P("kv", None, "pb"))
    return jax.shard_map(shards, mesh=mesh, in_specs=in_specs, out_specs=out_specs, check_vma=False)
```

```python
import functools
import math

import jax
import jax.numpy as jnp
from jax import lax
from jax.experimental import pallas as pl
from jax.experimental.pallas import tpu as pltpu
from jax.sharding import PartitionSpec as P

eps = 1e-06
LOG2E = math.log2(math.e)
F32, F16, BF16 = jnp.float32, jnp.float16, jnp.bfloat16
VMEM = pl.BlockSpec(memory_space=pltpu.VMEM)
ANY = pl.BlockSpec(memory_space=pl.ANY)
NT = (((1,), (1,)), ((), ()))
TT = (((0,), (0,)), ((), ()))
STAT = 8
FIRST = 12


def call(name, body, outs, ins, scratch=(), after=(), specs=(), flops=0, exps=0, moved=0, limit=20):
    count, skip = len(ins), len(after)

    def ordered(*refs):
        body(*refs[:count], *refs[count + skip :])

    return pl.pallas_call(
        ordered,
        name=name,
        out_shape=[jax.ShapeDtypeStruct(s, d) for s, d in outs],
        in_specs=(list(specs) or [VMEM] * count) + [ANY] * skip,
        out_specs=[VMEM] * len(outs),
        scratch_shapes=list(scratch),
        compiler_params=pltpu.CompilerParams(vmem_limit_bytes=int(limit * 2**20)),
        cost_estimate=pl.CostEstimate(flops=flops, transcendentals=exps, bytes_accessed=moved),
    )(*ins, *after)


def split3(x):
    hi = x.astype(BF16)
    rest = x - hi.astype(F32)
    mid = rest.astype(BF16)
    low = (rest - mid.astype(F32)).astype(BF16)
    return hi, mid, low


def joined3(a, b, c):
    return (a.astype(F32) + b.astype(F32)) + c.astype(F32)


def packed3(line):
    hi, mid, low = split3(jnp.broadcast_to(line, (STAT, 128)))
    r = lax.broadcasted_iota(jnp.int32, (STAT, 128), 0)
    return jnp.where(r == 0, hi.astype(F32), jnp.where(r == 1, mid.astype(F32), low.astype(F32))).astype(BF16)


def column(line):
    return jnp.broadcast_to(line, (128, 128)).T


def slot(z, ring):
    return (z - FIRST) % ring


def place(ring):
    at = lax.axis_index("ctx")
    return at // ring, at % ring


def select(sel_ref, k_ref, pick_ref):
    half, width = pick_ref.shape
    count = sel_ref.shape[1]
    tokens = k_ref.shape[0]
    base = lax.axis_index("ctx") * tokens
    first = lax.axis_index("pb") * half
    row = lax.broadcasted_iota(jnp.int32, (half, count), 0) + first
    lane = lax.broadcasted_iota(jnp.int32, (half, count), 1)
    sel = jnp.broadcast_to((sel_ref[...] - base).astype(F32), (half, count))
    col = jnp.sum(jnp.where(row == lane, sel, 0.0), axis=1, keepdims=True).astype(jnp.int32)
    step = 512
    acc = jnp.zeros((half, width), F32)
    for k in range(0, tokens, step):
        at = lax.broadcasted_iota(jnp.int32, (half, step), 1) + k
        hot = (at == col).astype(F32).astype(BF16)
        acc += jnp.dot(hot, k_ref[k : k + step, :], preferred_element_type=F32)
    pick_ref[...] = acc


def attend(ring, away, q_hbm, k_hbm, v_hbm, q_ref, k_ref, v_ref, s_ref, sem, fetch=None, pick=None):
    rows, width = q_ref.shape
    tokens = k_ref.shape[0]
    step = 512
    c = LOG2E * width**-0.5
    x, _ = place(ring)
    part = 1 - x if away else x
    copies = [pltpu.make_async_copy(q_hbm.at[pl.ds(pl.multiple_of(part * rows, rows), rows)], q_ref, sem.at[0])]
    cuts = [pl.ds(0, tokens // 4), pl.ds(tokens // 4, tokens - tokens // 4)]
    copies += [pltpu.make_async_copy(k_hbm.at[cut], k_ref.at[cut], sem.at[1 + n]) for n, cut in enumerate(cuts)]
    copies.append(pltpu.make_async_copy(v_hbm, v_ref, sem.at[3]))
    for copy in copies:
        copy.start()
    copies[0].wait()
    copies[1].wait()
    q = q_ref[...]
    mx = None
    for a in range(0, tokens, step):
        if a == tokens // 4:
            copies[2].wait()
            if fetch is not None:
                fetch.wait()
        s = lax.dot_general(k_ref[a : a + step, :], q, NT, preferred_element_type=F32)
        s_ref[a : a + step, :] = s
        top = jnp.max(s.reshape(step // 8, 8, rows), axis=0)
        mx = top if mx is None else jnp.maximum(mx, top)
    mc = jnp.max(mx, axis=0, keepdims=True) * c
    if pick is not None:
        pick()
    total, out = jnp.zeros((8, rows), F32), jnp.zeros((width, rows), F32)
    copies[3].wait()
    for a in range(0, tokens, step):
        p = jnp.exp2(s_ref[a : a + step, :] * c - mc)
        total = total + jnp.sum(p.reshape(step // 8, 8, rows), axis=0)
        out = out + lax.dot_general(v_ref[a : a + step, :], p.astype(BF16), TT, preferred_element_type=F32)
    total = jnp.sum(total, axis=0, keepdims=True)
    return (out * (1.0 / total)).T, (mc + jnp.log2(total)) * (1.0 / LOG2E)


def away_body(ring, sel_hbm, q_hbm, k_hbm, v_hbm, out_ref, pick_ref, sel_ref, q_ref, k_ref, v_ref, s_ref, sem, sel_sem):
    fetch = pltpu.make_async_copy(sel_hbm, sel_ref, sel_sem)
    fetch.start()

    def pick():
        select(sel_ref, k_ref, pick_ref)
        out_ref[ring, : pick_ref.shape[0], :] = pick_ref[...]

    o, lse = attend(ring, True, q_hbm, k_hbm, v_hbm, q_ref, k_ref, v_ref, s_ref, sem, fetch, pick)
    rows = q_ref.shape[0]
    share = rows // ring
    per = 128 // share
    for g in range(rows // 128):
        three = packed3(lse[:, g * 128 : (g + 1) * 128]).astype(F32)
        for j in range(g * per, (g + 1) * per):
            out_ref[j, :share, :] = o[j * share : (j + 1) * share, :]
            out_ref[j, share:, :] = three


def home_body(ring, q_hbm, k_hbm, v_hbm, out_ref, lse_ref, q_ref, k_ref, v_ref, s_ref, sem):
    o, lse = attend(ring, False, q_hbm, k_hbm, v_hbm, q_ref, k_ref, v_ref, s_ref, sem)
    out_ref[...] = o
    lse_ref[...] = jnp.zeros_like(lse_ref)
    for g in range(o.shape[0] // 128):
        lse_ref[g : g + 1, :] = lse[:, g * 128 : (g + 1) * 128]


def pair_body(o_ref, lse_ref, in_ref, pick_ref, out_ref):
    ring, length, _ = out_ref.shape
    rows = o_ref.shape[0]
    half = pick_ref.shape[0]
    share = rows // ring
    per = 128 // share
    mine, theirs = pick_ref[...], in_ref[ring, :half, :]
    for g in range(rows // 128):
        three = in_ref[g * per, share:, :]
        other = (three[0:1] + three[1:2]) + three[2:3]
        here = lse_ref[g : g + 1, :]
        top = jnp.maximum(other, here)
        wo, wh = jnp.exp(other - top), jnp.exp(here - top)
        total = wo + wh
        lines = packed3(top + jnp.log(total))
        share_of = column(wh / total)
        for j in range(g * per, (g + 1) * per):
            w = share_of[(j % per) * share : (j % per + 1) * share, :]
            a = in_ref[j, :share, :]
            h = o_ref[j * share : (j + 1) * share, :]
            to = slot(j, ring)
            out_ref[to, :share, :] = a + w * (h - a)
            out_ref[to, share : share + half, :] = mine
            out_ref[to, share + half : length - STAT, :] = theirs
            out_ref[to, length - STAT :, :] = lines.astype(F32)


def settle_body(share, in_ref, out_ref, keys_ref, w_ref):
    ring, length, _ = in_ref.shape
    _, z = place(ring)
    lines = in_ref[:, length - STAT :, :]
    lse = (lines[:, 0, :] + lines[:, 1, :]) + lines[:, 2, :]
    top = jnp.max(lse, axis=0, keepdims=True)
    w = jnp.exp(lse - top)
    total = jnp.sum(w, axis=0, keepdims=True)
    w = w / total
    w_ref[...] = jnp.concatenate([w, jnp.zeros((128 - ring, 128), F32)], axis=0).T
    mine = w_ref[pl.ds(pl.multiple_of((z % (128 // share)) * share, share), share), :]
    acc = jnp.zeros((share, 128), F32)
    for b in range(ring):
        acc = acc + mine[:, b : b + 1] * in_ref[b, :share, :]
    y = (acc * lax.rsqrt(jnp.mean(acc * acc, axis=1, keepdims=True) + eps)).astype(BF16)
    three = packed3(top + jnp.log(total))
    for p in range(ring):
        out_ref[p, :share, :] = y
        out_ref[p, share:, :] = three
        keys_ref[p] = in_ref[p, share : length - STAT, :].astype(BF16)


def features_body(rt, q_ref, mine_ref, other_ref, own_ref, stat_ref, keep_ref, send_ref, c_ref, f_ref, g_ref):
    rows, width = q_ref.shape
    ring, count, _ = mine_ref.shape
    half = count // 2
    sel = 2 * ring * count
    c = LOG2E * width**-0.5
    pb = lax.axis_index("pb")
    x, z = place(ring)
    for j in range(ring):
        for ref, core in ((mine_ref, pb), (other_ref, 1 - pb)):
            for k, side in ((0, x), (1, 1 - x)):
                at = pl.multiple_of((side * ring + j) * count + core * half, half)
                c_ref[pl.ds(at, half), :] = ref[slot(j, ring), k * half : (k + 1) * half, :]
    for t in range(rows // rt):
        s = lax.dot_general(c_ref[...], q_ref[t * rt : (t + 1) * rt, :], NT, preferred_element_type=F32)
        mx = jnp.max(s, axis=0, keepdims=True) * c
        e = jnp.exp2(s * c - mx)
        total = jnp.sum(e, axis=0, keepdims=True)
        f_ref[:, t * rt : (t + 1) * rt] = (e * (sel / total)).astype(BF16)
        stat = (mx + jnp.log2(total)) * (1.0 / LOG2E)
        for g in range(rt // 128):
            r = t * (rt // 128) + g
            stat_ref[r : r + 1, :] = stat[:, g * 128 : (g + 1) * 128]
    there = rows // 2
    lanes = pl.ds(pl.multiple_of(x * there, there), there)
    for k, side in ((0, x), (1, 1 - x)):
        at = pl.multiple_of((side * ring + z) * count, count)
        own_ref[k * count : (k + 1) * count, :] = f_ref[pl.ds(at, count), lanes]
    at = lax.axis_index("ctx") * count
    g_ref[:half, :] = f_ref[pl.ds(pl.multiple_of(at + pb * half, half), half), :]
    g_ref[half:, :] = f_ref[pl.ds(pl.multiple_of(at + (1 - pb) * half, half), half), :]
    step = 512
    for k in range(0, sel, step):
        g = lax.dot_general(g_ref[...], f_ref[k : k + step, :], NT, preferred_element_type=F32)
        g = g * (1.0 / (2 * rows))
        keep_ref[:, k : k + step] = g[:half]
        send_ref[:, k : k + step] = g[half:]


def rhs_body(total_rows, in_ref, own_ref, send_ref, y_ref, g_ref):
    ring, block, _ = in_ref.shape
    share = block - STAT
    half = send_ref.shape[1] - 8
    rows = ring * share
    x, _ = place(ring)
    for p in range(ring):
        y_ref[p * share : (p + 1) * share, :] = in_ref[slot(p, ring), :share, :]
    g_ref[...] = jnp.dot(own_ref[...], y_ref[...], preferred_element_type=F32) * (1.0 / total_rows)
    per = 128 // share
    lane = lax.broadcasted_iota(jnp.int32, (1, 128), 1)
    lines = []
    for h in range(rows // 128):
        line = jnp.zeros((1, 128), F32)
        for j in range(per):
            v = in_ref[slot(h * per + j, ring), share:, :].astype(F32)
            v = (v[0:1] + v[1:2]) + v[2:3]
            line = jnp.where((lane >= j * share) & (lane < (j + 1) * share), v, line)
        lines.append(line)
    lines = jnp.concatenate(lines + [jnp.zeros((8 - len(lines), 128), F32)], axis=0)
    for k in range(4):
        other = x if k < 2 else 1 - x
        send_ref[k, :half, :] = g_ref[pl.ds(pl.multiple_of(other * (2 * half) + (k % 2) * half, half), half), :]
        send_ref[k, half:, :] = lines


def last_body(got_ref, stat_ref, keep_ref, in_ref, gram_ref, rhs_ref, gap_ref):
    half = rhs_ref.shape[0]
    rhs_ref[...] = (got_ref[0, :half, :] + got_ref[1, :half, :]) + (got_ref[2, :half, :] + got_ref[3, :half, :])
    gram_ref[...] = keep_ref[...] + in_ref[...]
    pb = lax.axis_index("pb")
    lines = gap_ref.shape[0] // 2
    gap_ref[:lines, :] = got_ref[pb, half : half + lines, :] - stat_ref[:lines, :]
    gap_ref[lines:, :] = got_ref[2 + pb, half : half + lines, :] - stat_ref[lines:, :]


def shards(queries, cache_keys, cache_values, sel_index):
    heads, rows_dev, width = queries.shape[1:]
    q = queries[0].reshape(-1, width)
    keys, values = cache_keys[0], cache_values[0]
    rows, tokens = q.shape[0], keys.shape[0]
    blocks = lax.axis_size("ctx")
    ring = blocks // 2
    part = rows // 2
    share = part // ring
    block = share + STAT
    count = sel_index.shape[1]
    half = count // 2
    sel = count * blocks
    total_rows = 2 * rows
    swap = [(0, 1), (1, 0)]
    across = [(i, (i + ring) % blocks) for i in range(blocks)]
    rings = [[side + (j + FIRST) % ring for j in range(ring)] for side in (0, ring)]

    def exchange(x):
        return lax.all_to_all(x, "ctx", 0, 0, axis_index_groups=rings, tiled=True)

    held = [
        pltpu.VMEM((part, width), BF16),
        pltpu.VMEM((tokens, width), BF16),
        pltpu.VMEM((tokens, width), BF16),
        pltpu.VMEM((tokens, part), F32),
        pltpu.SemaphoreType.DMA((4,)),
    ]
    work = dict(flops=4 * part * tokens * width, exps=part * tokens, moved=tokens * width * 4, limit=60.0)
    away, picked = call(
        "away",
        functools.partial(away_body, ring),
        [((ring + 1, block, width), F32), ((half, width), F32)],
        (sel_index, q, keys, values),
        specs=[ANY] * 4,
        scratch=[pltpu.VMEM((1, count), jnp.int32), *held, pltpu.SemaphoreType.DMA],
        **work,
    )
    came = lax.ppermute(away.astype(F16), "ctx", across).astype(F32)
    home, lse = call(
        "home",
        functools.partial(home_body, ring),
        [((part, width), F32), ((8, 128), F32)],
        (q, keys, values),
        specs=[ANY] * 3,
        scratch=held,
        **(work | dict(limit=53.5)),
    )
    (parts,) = call("pair", pair_body, [((ring, block + count, width), F32)], (home, lse, came, picked), moved=part * width * 12)
    told, mine = call(
        "settle",
        functools.partial(settle_body, share),
        [((ring, block, width), BF16), ((ring, count, width), BF16)],
        (exchange(parts.astype(F16)).astype(F32),),
        scratch=[pltpu.VMEM((128, 128), F32)],
        moved=part * width * 8,
    )
    heard = exchange(told)
    other = lax.ppermute(mine, "pb", swap)
    own, stat, gkeep, gsend = call(
        "features",
        functools.partial(features_body, 256),
        [((2 * count, part), BF16), ((rows // 128, 128), F32), ((half, sel), F32), ((half, sel), F32)],
        (q, mine, other),
        after=(told,),
        scratch=[pltpu.VMEM((sel, width), BF16), pltpu.VMEM((sel, rows), BF16), pltpu.VMEM((count, rows), BF16)],
        flops=2 * rows * sel * (width + count),
        exps=rows * sel,
        moved=sel * width * 4,
    )
    quads = [[2 * (side + z) + core for side in (0, ring) for core in (0, 1)] for z in range(ring)]
    (send,) = call(
        "rhs",
        functools.partial(rhs_body, total_rows),
        [((4, half + 8, width), F32)],
        (heard, own),
        scratch=[pltpu.VMEM((part, width), BF16), pltpu.VMEM((2 * count, width), F32)],
        flops=4 * count * part * width,
        moved=part * width * 2,
    )
    got = lax.all_to_all(send, ("ctx", "pb"), 0, 0, axis_index_groups=quads, tiled=True)
    gram, rhs, gap = call(
        "last",
        last_body,
        [((half, sel), F32), ((half, width), F32), ((rows // 128, 128), F32)],
        (got, stat, gkeep, lax.ppermute(gsend, "pb", swap)),
        moved=half * sel * 12,
    )
    return (gram[None], rhs[None], gap.reshape(1, heads, rows_dev))


def solution(mesh):
    in_specs = (
        P("kv", None, "pb", None),
        P("kv", "ctx", None),
        P("kv", "ctx", None),
        P("kv", "ctx"),
    )
    out_specs = (P("kv", ("ctx", "pb"), None), P("kv", ("ctx", "pb"), None), P("kv", None, "pb"))
    return jax.shard_map(shards, mesh=mesh, in_specs=in_specs, out_specs=out_specs, check_vma=False)
```

```python
import functools
import math

import jax
import jax.numpy as jnp
from jax import lax
from jax.experimental import pallas as pl
from jax.experimental.pallas import tpu as pltpu
from jax.sharding import PartitionSpec as P

eps = 1e-06
LOG2E = math.log2(math.e)
F32, F16, BF16 = jnp.float32, jnp.float16, jnp.bfloat16
VMEM = pl.BlockSpec(memory_space=pltpu.VMEM)
ANY = pl.BlockSpec(memory_space=pl.ANY)
NT = (((1,), (1,)), ((), ()))
TT = (((0,), (0,)), ((), ()))
STAT = 8
FIRST = 12


def call(name, body, outs, ins, scratch=(), after=(), specs=(), flops=0, exps=0, moved=0, limit=20):
    count, skip = len(ins), len(after)

    def ordered(*refs):
        body(*refs[:count], *refs[count + skip :])

    return pl.pallas_call(
        ordered,
        name=name,
        out_shape=[jax.ShapeDtypeStruct(s, d) for s, d in outs],
        in_specs=(list(specs) or [VMEM] * count) + [ANY] * skip,
        out_specs=[VMEM] * len(outs),
        scratch_shapes=list(scratch),
        compiler_params=pltpu.CompilerParams(vmem_limit_bytes=int(limit * 2**20)),
        cost_estimate=pl.CostEstimate(flops=flops, transcendentals=exps, bytes_accessed=moved),
    )(*ins, *after)


def split3(x):
    hi = x.astype(BF16)
    rest = x - hi.astype(F32)
    mid = rest.astype(BF16)
    low = (rest - mid.astype(F32)).astype(BF16)
    return hi, mid, low


def joined3(a, b, c):
    return (a.astype(F32) + b.astype(F32)) + c.astype(F32)


def packed3(line):
    hi, mid, low = split3(jnp.broadcast_to(line, (STAT, 128)))
    r = lax.broadcasted_iota(jnp.int32, (STAT, 128), 0)
    return jnp.where(r == 0, hi.astype(F32), jnp.where(r == 1, mid.astype(F32), low.astype(F32))).astype(BF16)


def column(line):
    return jnp.broadcast_to(line, (128, 128)).T


def slot(z, ring):
    return (z - FIRST) % ring


def place(ring):
    at = lax.axis_index("ctx")
    return at // ring, at % ring


def select(sel_ref, k_ref, pick_ref):
    half, width = pick_ref.shape
    count = sel_ref.shape[1]
    tokens = k_ref.shape[0]
    base = lax.axis_index("ctx") * tokens
    first = lax.axis_index("pb") * half
    row = lax.broadcasted_iota(jnp.int32, (half, count), 0) + first
    lane = lax.broadcasted_iota(jnp.int32, (half, count), 1)
    sel = jnp.broadcast_to((sel_ref[...] - base).astype(F32), (half, count))
    col = jnp.sum(jnp.where(row == lane, sel, 0.0), axis=1, keepdims=True).astype(jnp.int32)
    step = 512
    acc = jnp.zeros((half, width), F32)
    for k in range(0, tokens, step):
        at = lax.broadcasted_iota(jnp.int32, (half, step), 1) + k
        hot = (at == col).astype(F32).astype(BF16)
        acc += jnp.dot(hot, k_ref[k : k + step, :], preferred_element_type=F32)
    pick_ref[...] = acc


def attend(ring, away, q_hbm, k_hbm, v_hbm, q_ref, k_ref, v_ref, s_ref, sem, fetch=None, pick=None):
    rows, width = q_ref.shape
    tokens = k_ref.shape[0]
    step = 512
    c = LOG2E * width**-0.5
    x, _ = place(ring)
    part = 1 - x if away else x
    copies = [pltpu.make_async_copy(q_hbm.at[pl.ds(pl.multiple_of(part * rows, rows), rows)], q_ref, sem.at[0])]
    copies += [pltpu.make_async_copy(k_hbm, k_ref, sem.at[1]), pltpu.make_async_copy(v_hbm, v_ref, sem.at[2])]
    for copy in copies:
        copy.start()
    copies[0].wait()
    copies[1].wait()
    if fetch is not None:
        fetch.wait()
    q = q_ref[...]
    mx = None
    for a in range(0, tokens, step):
        s = lax.dot_general(k_ref[a : a + step, :], q, NT, preferred_element_type=F32)
        s_ref[a : a + step, :] = s
        top = jnp.max(s.reshape(step // 8, 8, rows), axis=0)
        mx = top if mx is None else jnp.maximum(mx, top)
    mc = jnp.max(mx, axis=0, keepdims=True) * c
    if pick is not None:
        pick()
    total, out = jnp.zeros((8, rows), F32), jnp.zeros((width, rows), F32)
    copies[2].wait()
    for a in range(0, tokens, step):
        p = jnp.exp2(s_ref[a : a + step, :] * c - mc)
        total = total + jnp.sum(p.reshape(step // 8, 8, rows), axis=0)
        out = out + lax.dot_general(v_ref[a : a + step, :], p.astype(BF16), TT, preferred_element_type=F32)
    total = jnp.sum(total, axis=0, keepdims=True)
    return (out * (1.0 / total)).T, (mc + jnp.log2(total)) * (1.0 / LOG2E)


def away_body(ring, sel_hbm, q_hbm, k_hbm, v_hbm, out_ref, pick_ref, sel_ref, q_ref, k_ref, v_ref, s_ref, sem, sel_sem):
    fetch = pltpu.make_async_copy(sel_hbm, sel_ref, sel_sem)
    fetch.start()

    def pick():
        select(sel_ref, k_ref, pick_ref)
        out_ref[ring, : pick_ref.shape[0], :] = pick_ref[...]

    o, lse = attend(ring, True, q_hbm, k_hbm, v_hbm, q_ref, k_ref, v_ref, s_ref, sem, fetch, pick)
    rows = q_ref.shape[0]
    share = rows // ring
    per = 128 // share
    for g in range(rows // 128):
        three = packed3(lse[:, g * 128 : (g + 1) * 128]).astype(F32)
        for j in range(g * per, (g + 1) * per):
            out_ref[j, :share, :] = o[j * share : (j + 1) * share, :]
            out_ref[j, share:, :] = three


def home_body(ring, q_hbm, k_hbm, v_hbm, out_ref, lse_ref, q_ref, k_ref, v_ref, s_ref, sem):
    o, lse = attend(ring, False, q_hbm, k_hbm, v_hbm, q_ref, k_ref, v_ref, s_ref, sem)
    out_ref[...] = o
    lse_ref[...] = jnp.zeros_like(lse_ref)
    for g in range(o.shape[0] // 128):
        lse_ref[g : g + 1, :] = lse[:, g * 128 : (g + 1) * 128]


def pair_body(o_ref, lse_ref, in_ref, pick_ref, out_ref):
    ring, length, _ = out_ref.shape
    rows = o_ref.shape[0]
    half = pick_ref.shape[0]
    share = rows // ring
    per = 128 // share
    mine, theirs = pick_ref[...], in_ref[ring, :half, :]
    for g in range(rows // 128):
        three = in_ref[g * per, share:, :]
        other = (three[0:1] + three[1:2]) + three[2:3]
        here = lse_ref[g : g + 1, :]
        top = jnp.maximum(other, here)
        wo, wh = jnp.exp(other - top), jnp.exp(here - top)
        total = wo + wh
        lines = packed3(top + jnp.log(total))
        share_of = column(wh / total)
        for j in range(g * per, (g + 1) * per):
            w = share_of[(j % per) * share : (j % per + 1) * share, :]
            a = in_ref[j, :share, :]
            h = o_ref[j * share : (j + 1) * share, :]
            to = slot(j, ring)
            out_ref[to, :share, :] = a + w * (h - a)
            out_ref[to, share : share + half, :] = mine
            out_ref[to, share + half : length - STAT, :] = theirs
            out_ref[to, length - STAT :, :] = lines.astype(F32)


def settle_body(share, in_ref, out_ref, keys_ref, w_ref):
    ring, length, _ = in_ref.shape
    _, z = place(ring)
    lines = in_ref[:, length - STAT :, :]
    lse = (lines[:, 0, :] + lines[:, 1, :]) + lines[:, 2, :]
    top = jnp.max(lse, axis=0, keepdims=True)
    w = jnp.exp(lse - top)
    total = jnp.sum(w, axis=0, keepdims=True)
    w = w / total
    w_ref[...] = jnp.concatenate([w, jnp.zeros((128 - ring, 128), F32)], axis=0).T
    mine = w_ref[pl.ds(pl.multiple_of((z % (128 // share)) * share, share), share), :]
    acc = jnp.zeros((share, 128), F32)
    for b in range(ring):
        acc = acc + mine[:, b : b + 1] * in_ref[b, :share, :]
    y = (acc * lax.rsqrt(jnp.mean(acc * acc, axis=1, keepdims=True) + eps)).astype(BF16)
    three = packed3(top + jnp.log(total))
    for p in range(ring):
        out_ref[p, :share, :] = y
        out_ref[p, share:, :] = three
        keys_ref[p] = in_ref[p, share : length - STAT, :].astype(BF16)


def features_body(rt, q_ref, mine_ref, other_ref, own_ref, stat_ref, keep_ref, send_ref, c_ref, f_ref, g_ref):
    rows, width = q_ref.shape
    ring, count, _ = mine_ref.shape
    half = count // 2
    sel = 2 * ring * count
    c = LOG2E * width**-0.5
    pb = lax.axis_index("pb")
    x, z = place(ring)
    for j in range(ring):
        for ref, core in ((mine_ref, pb), (other_ref, 1 - pb)):
            for k, side in ((0, x), (1, 1 - x)):
                at = pl.multiple_of((side * ring + j) * count + core * half, half)
                c_ref[pl.ds(at, half), :] = ref[slot(j, ring), k * half : (k + 1) * half, :]
    for t in range(rows // rt):
        s = lax.dot_general(c_ref[...], q_ref[t * rt : (t + 1) * rt, :], NT, preferred_element_type=F32)
        mx = jnp.max(s, axis=0, keepdims=True) * c
        e = jnp.exp2(s * c - mx)
        total = jnp.sum(e, axis=0, keepdims=True)
        f_ref[:, t * rt : (t + 1) * rt] = (e * (sel / total)).astype(BF16)
        stat = (mx + jnp.log2(total)) * (1.0 / LOG2E)
        for g in range(rt // 128):
            r = t * (rt // 128) + g
            stat_ref[r : r + 1, :] = stat[:, g * 128 : (g + 1) * 128]
    there = rows // 2
    lanes = pl.ds(pl.multiple_of(x * there, there), there)
    for k, side in ((0, x), (1, 1 - x)):
        at = pl.multiple_of((side * ring + z) * count, count)
        own_ref[k * count : (k + 1) * count, :] = f_ref[pl.ds(at, count), lanes]
    at = lax.axis_index("ctx") * count
    g_ref[:half, :] = f_ref[pl.ds(pl.multiple_of(at + pb * half, half), half), :]
    g_ref[half:, :] = f_ref[pl.ds(pl.multiple_of(at + (1 - pb) * half, half), half), :]
    step = 512
    for k in range(0, sel, step):
        g = lax.dot_general(g_ref[...], f_ref[k : k + step, :], NT, preferred_element_type=F32)
        g = g * (1.0 / (2 * rows))
        keep_ref[:, k : k + step] = g[:half]
        send_ref[:, k : k + step] = g[half:]


def rhs_body(total_rows, in_ref, own_ref, send_ref, y_ref, g_ref):
    ring, block, _ = in_ref.shape
    share = block - STAT
    half = send_ref.shape[1] - 8
    rows = ring * share
    x, _ = place(ring)
    for p in range(ring):
        y_ref[p * share : (p + 1) * share, :] = in_ref[slot(p, ring), :share, :]
    g_ref[...] = jnp.dot(own_ref[...], y_ref[...], preferred_element_type=F32) * (1.0 / total_rows)
    per = 128 // share
    lane = lax.broadcasted_iota(jnp.int32, (1, 128), 1)
    lines = []
    for h in range(rows // 128):
        line = jnp.zeros((1, 128), F32)
        for j in range(per):
            v = in_ref[slot(h * per + j, ring), share:, :].astype(F32)
            v = (v[0:1] + v[1:2]) + v[2:3]
            line = jnp.where((lane >= j * share) & (lane < (j + 1) * share), v, line)
        lines.append(line)
    lines = jnp.concatenate(lines + [jnp.zeros((8 - len(lines), 128), F32)], axis=0)
    for k in range(4):
        other = x if k < 2 else 1 - x
        send_ref[k, :half, :] = g_ref[pl.ds(pl.multiple_of(other * (2 * half) + (k % 2) * half, half), half), :]
        send_ref[k, half:, :] = lines


def last_body(got_ref, stat_ref, keep_ref, in_ref, gram_ref, rhs_ref, gap_ref):
    half = rhs_ref.shape[0]
    rhs_ref[...] = (got_ref[0, :half, :] + got_ref[1, :half, :]) + (got_ref[2, :half, :] + got_ref[3, :half, :])
    gram_ref[...] = keep_ref[...] + in_ref[...]
    pb = lax.axis_index("pb")
    lines = gap_ref.shape[0] // 2
    gap_ref[:lines, :] = got_ref[pb, half : half + lines, :] - stat_ref[:lines, :]
    gap_ref[lines:, :] = got_ref[2 + pb, half : half + lines, :] - stat_ref[lines:, :]


def shards(queries, cache_keys, cache_values, sel_index):
    heads, rows_dev, width = queries.shape[1:]
    q = queries[0].reshape(-1, width)
    keys, values = cache_keys[0], cache_values[0]
    rows, tokens = q.shape[0], keys.shape[0]
    blocks = lax.axis_size("ctx")
    ring = blocks // 2
    part = rows // 2
    share = part // ring
    block = share + STAT
    count = sel_index.shape[1]
    half = count // 2
    sel = count * blocks
    total_rows = 2 * rows
    swap = [(0, 1), (1, 0)]
    across = [(i, (i + ring) % blocks) for i in range(blocks)]
    rings = [[side + (j + FIRST) % ring for j in range(ring)] for side in (0, ring)]

    def exchange(x):
        return lax.all_to_all(x, "ctx", 0, 0, axis_index_groups=rings, tiled=True)

    held = [
        pltpu.VMEM((part, width), BF16),
        pltpu.VMEM((tokens, width), BF16),
        pltpu.VMEM((tokens, width), BF16),
        pltpu.VMEM((tokens, part), F32),
        pltpu.SemaphoreType.DMA((3,)),
    ]
    work = dict(flops=4 * part * tokens * width, exps=part * tokens, moved=tokens * width * 4, limit=60.0)
    away, picked = call(
        "away",
        functools.partial(away_body, ring),
        [((ring + 1, block, width), F32), ((half, width), F32)],
        (sel_index, q, keys, values),
        specs=[ANY] * 4,
        scratch=[pltpu.VMEM((1, count), jnp.int32), *held, pltpu.SemaphoreType.DMA],
        **work,
    )
    came = lax.ppermute(away.astype(F16), "ctx", across).astype(F32)
    home, lse = call(
        "home",
        functools.partial(home_body, ring),
        [((part, width), F32), ((8, 128), F32)],
        (q, keys, values),
        specs=[ANY] * 3,
        scratch=held,
        **(work | dict(limit=53.5)),
    )
    (parts,) = call("pair", pair_body, [((ring, block + count, width), F32)], (home, lse, came, picked), moved=part * width * 12)
    told, mine = call(
        "settle",
        functools.partial(settle_body, share),
        [((ring, block, width), BF16), ((ring, count, width), BF16)],
        (exchange(parts.astype(F16)).astype(F32),),
        scratch=[pltpu.VMEM((128, 128), F32)],
        moved=part * width * 8,
    )
    heard = exchange(told)
    other = lax.ppermute(mine, "pb", swap)
    own, stat, gkeep, gsend = call(
        "features",
        functools.partial(features_body, 512),
        [((2 * count, part), BF16), ((rows // 128, 128), F32), ((half, sel), F32), ((half, sel), F32)],
        (q, mine, other),
        after=(told,),
        scratch=[pltpu.VMEM((sel, width), BF16), pltpu.VMEM((sel, rows), BF16), pltpu.VMEM((count, rows), BF16)],
        flops=2 * rows * sel * (width + count),
        exps=rows * sel,
        moved=sel * width * 4,
    )
    quads = [[2 * (side + z) + core for side in (0, ring) for core in (0, 1)] for z in range(ring)]
    (send,) = call(
        "rhs",
        functools.partial(rhs_body, total_rows),
        [((4, half + 8, width), F32)],
        (heard, own),
        scratch=[pltpu.VMEM((part, width), BF16), pltpu.VMEM((2 * count, width), F32)],
        flops=4 * count * part * width,
        moved=part * width * 2,
    )
    got = lax.all_to_all(send, ("ctx", "pb"), 0, 0, axis_index_groups=quads, tiled=True)
    gram, rhs, gap = call(
        "last",
        last_body,
        [((half, sel), F32), ((half, width), F32), ((rows // 128, 128), F32)],
        (got, stat, gkeep, lax.ppermute(gsend, "pb", swap)),
        moved=half * sel * 12,
    )
    return (gram[None], rhs[None], gap.reshape(1, heads, rows_dev))


def solution(mesh):
    in_specs = (
        P("kv", None, "pb", None),
        P("kv", "ctx", None),
        P("kv", "ctx", None),
        P("kv", "ctx"),
    )
    out_specs = (P("kv", ("ctx", "pb"), None), P("kv", ("ctx", "pb"), None), P("kv", None, "pb"))
    return jax.shard_map(shards, mesh=mesh, in_specs=in_specs, out_specs=out_specs, check_vma=False)
```
